32 devices in a mesh: layer: 4 (over x, core), feat: 8 (over z, y).
Axes of the slice: x: 2, y: 2, z: 4, core: 2. Of those that a mesh axis runs over, the one named last changes fastest.
Arguments:
- layer_acts: bfloat16 [4, 512, 576], P('layer', 'feat'), may hold values from -6 to 6
- enc_weight: bfloat16 [4, 576, 16384], P('layer', None, 'feat'), may hold values from -6 to 6
- dec_weight: bfloat16 [4, 16384, 576], P('layer', 'feat'), may hold values from -6 to 6
- enc_bias: float32 [16384], P('feat'), may hold values from -4 to 4
- dec_bias: float32 [4, 576], P('layer'), may hold values from -4 to 4
Outputs:
- enc_step: bfloat16 [4, 576, 16384], P('layer', None, 'feat')
- dec_step: bfloat16 [4, 16384, 576], P('layer', 'feat')
The draws below stay inside these ranges and needn't reach their ends.
All inputs are finite; a program needn't handle non-finite values.
Results may differ from the reference program's by a relative error of at most 0.012.
Values may be sent and summed in bfloat16 or wider, within the bound.
A program may use at most 64 MiB of HBM per device.

```python
import jax
import jax.numpy as jnp
from jax import lax

D = 576
F_DEV = 2048
TOKENS = 512
LAYERS = 4
FEATURES = 16384


def shard_levels(stream_key, shape, cuts, smallest, high):
    def one(dim, blocks):
        heights = jax.random.uniform(jax.random.fold_in(jax.random.fold_in(stream_key, 6), dim), (blocks,), jnp.float32, smallest / len(cuts), high / len(cuts))
        return jnp.repeat(jnp.exp(heights), shape[dim] // blocks).reshape((-1,) + (1,) * (len(shape) - dim - 1))

    factor_of = one(*cuts[0])
    for cut in cuts[1:]:
        factor_of = factor_of * one(*cut)
    return factor_of


def gaussian(rng, shape, deviation, reach, cuts=(), dtype=jnp.bfloat16):
    gain = shard_levels(rng, shape, cuts, -0.22, 0.18) if cuts else 1.0
    drawn = jax.random.normal(rng, shape, jnp.float32) * deviation * gain
    return jnp.minimum(jnp.maximum(drawn, -reach), reach).astype(dtype)


def setup_inputs(seed: int = 0) -> dict:
    keys = jax.random.split(jax.random.key(seed), 6)
    return {
        "layer_acts": gaussian(keys[0], (LAYERS, TOKENS, D), 1.0, 6.0, ((0, 4), (1, 8))),
        "enc_weight": gaussian(keys[1], (LAYERS, D, FEATURES), 1.0, 6.0, ((0, 4), (2, 8))),
        "dec_weight": gaussian(keys[2], (LAYERS, FEATURES, D), 1.0, 6.0, ((0, 4), (1, 8))),
        "enc_bias": gaussian(keys[3], (FEATURES,), 0.7, 4.0, ((0, 8),), jnp.float32),
        "dec_bias": gaussian(keys[4], (LAYERS, D), 0.7, 4.0, ((0, 4),), jnp.float32),
    }


LEARN_RATE = 4.0


def contract_rows(left, right):
    return lax.dot_general(left, right, (((0,), (0,)), ((), ())), preferred_element_type=jnp.float32)


def reference(layer_acts, enc_weight, dec_weight, enc_bias, dec_bias):
    enc_scale = (LAYERS * D) ** -0.5
    dec_scale = FEATURES ** -0.5
    blocks = FEATURES // F_DEV
    enc_blocks = enc_weight.reshape(LAYERS, D, blocks, F_DEV).transpose(2, 0, 1, 3)
    dec_blocks = dec_weight.reshape(LAYERS, blocks, F_DEV, D).transpose(1, 0, 2, 3)
    bias_blocks = enc_bias.reshape(blocks, F_DEV)

    def encode(enc_block, bias_block):
        running = jnp.zeros((TOKENS, F_DEV), jnp.float32)
        for layer_index in range(LAYERS):
            running = running + jnp.dot(layer_acts[layer_index], enc_block[layer_index], preferred_element_type=jnp.float32)
        return enc_scale * running + bias_block

    def forward(recon, parts):
        enc_block, dec_block, bias_block = parts
        preact = encode(enc_block, bias_block)
        active_b = jnp.maximum(preact, 0.0).astype(jnp.bfloat16)
        decoded = jnp.stack([jnp.dot(active_b, dec_block[layer_index], preferred_element_type=jnp.float32) for layer_index in range(LAYERS)])
        return recon + dec_scale * decoded, None

    recon, unused = lax.scan(forward, jnp.zeros((LAYERS, TOKENS, D), jnp.float32), (enc_blocks, dec_blocks, bias_blocks))
    error_b = (recon + dec_bias[:, None, :] - layer_acts.astype(jnp.float32)).astype(jnp.bfloat16)

    def backward(parts):
        enc_block, dec_block, bias_block = parts
        preact = encode(enc_block, bias_block)
        active_b = jnp.maximum(preact, 0.0).astype(jnp.bfloat16)
        grad_dec = jnp.stack([contract_rows(active_b, error_b[layer_index]) for layer_index in range(LAYERS)])
        grad_act = jnp.zeros((TOKENS, F_DEV), jnp.float32)
        for layer_index in range(LAYERS):
            grad_act = grad_act + dec_scale * lax.dot_general(error_b[layer_index], dec_block[layer_index], (((1,), (1,)), ((), ())), preferred_element_type=jnp.float32)
        grad_pre = jnp.where(preact > 0.0, grad_act, 0.0).astype(jnp.bfloat16)
        grad_enc = jnp.stack([contract_rows(layer_acts[layer_index], grad_pre) for layer_index in range(LAYERS)])
        return (-LEARN_RATE * enc_scale * grad_enc).astype(jnp.bfloat16), (-LEARN_RATE * dec_scale * grad_dec).astype(jnp.bfloat16)

    enc_steps, dec_steps = lax.map(backward, (enc_blocks, dec_blocks, bias_blocks))
    enc_step = enc_steps.transpose(1, 2, 0, 3).reshape(LAYERS, D, FEATURES)
    dec_step = dec_steps.transpose(1, 0, 2, 3).reshape(LAYERS, FEATURES, D)
    return enc_step, dec_step
```

```python
import functools

import jax
import jax.numpy as jnp
from jax import lax
from jax.experimental import pallas as pl
from jax.experimental.pallas import tpu as pltpu
from jax.sharding import PartitionSpec as P

LEARN_RATE = 4.0
MESH = pl.DeviceIdType.MESH
F32 = jnp.float32
BF16 = jnp.bfloat16

STAGES = (
    ("partial", -6.0),
    ("pair_sum", 1.0),
    ("activate", 11.0),
    ("pass_active", 18.0),
    ("decode", 19.5),
    ("fold_y", 22.0),
    ("fold_z", 24.5),
    ("pass_error", 26.5),
    ("grad", 29.0),
    ("grad_pair", 31.0),
    ("mask", 40.0),
)
PERIOD = 8.0


def contract_rows(left, right):
    return lax.dot_general(left, right, (((0,), (0,)), ((), ())), preferred_element_type=F32)


def contract_columns(left, right):
    return lax.dot_general(left, right, (((1,), (1,)), ((), ())), preferred_element_type=F32)


def kernel(chunks, rows, quarter, enc_scale, dec_scale, tok_ref, enc_ref, dec_ref, bias_ref, dbias_ref,
           enc_out, dec_out, tok, psend, prec, pown, xsend, xrec, act, rpart, yrec, zsend, zrec, err,
           gsend, grec, gown, xgsend, xgrec, gp, sends, recvs):
    layer, feat = lax.axis_index("layer"), lax.axis_index("feat")
    xi, core = layer // 2, layer % 2
    zi, yi = feat // 2, feat % 2
    pair_dev = (xi * 2 + (1 - core), feat)
    x_dev = ((1 - xi) * 2 + core, feat)
    y_dev = (layer, zi * 2 + (1 - yi))

    def z_at(step):
        return lax.rem(zi + step + 4, 4)

    def z_dev(step):
        return (layer, z_at(step) * 2 + yi)

    barrier = pltpu.get_barrier_semaphore()
    peers = [pair_dev, x_dev, y_dev, z_dev(1), z_dev(2), z_dev(3)]
    for peer in peers:
        pl.semaphore_signal(barrier, inc=1, device_id=peer, device_id_type=MESH)
    pl.semaphore_wait(barrier, len(peers))

    started = []

    def copy(c, kind, src, dst, dev):
        return pltpu.make_async_remote_copy(
            src_ref=src, dst_ref=dst, send_sem=sends.at[c, kind], recv_sem=recvs.at[c, kind],
            device_id=dev, device_id_type=MESH)

    def send(c, kind, src, dst, dev):
        moving = copy(c, kind, src, dst, dev)
        moving.start()
        started.append(moving)

    def arrive(c, kind, dst, dev):
        copy(c, kind, dst, dst, dev).wait_recv()

    def gather_begin(c, base, buf):
        own = buf.at[c, feat]
        send(c, base, own, own, y_dev)
        for step in (1, 2, 3):
            send(c, base + step, own, own, z_dev(step))

    def gather_pass(c, base, buf):
        for step in (1, 3, 2):
            slot = buf.at[c, z_at(-step) * 2 + yi]
            arrive(c, base + step, slot, z_dev(-step))
            send(c, base + 3 + step, slot, slot, y_dev)

    def gather_end(c, base, buf):
        arrive(c, base, buf.at[c, zi * 2 + (1 - yi)], y_dev)
        for step in (1, 2, 3):
            arrive(c, base + 3 + step, buf.at[c, z_at(-step) * 2 + (1 - yi)], y_dev)

    TOK, ERR, PAIR, XP, XA, CA, CB, YR, ZR, GP, GX, GM = 0, 7, 14, 15, 16, 17, 18, 19, 20, 23, 24, 25

    def columns(q):
        return pl.ds(pl.multiple_of(q * quarter, quarter), quarter)

    def partial(c):
        if c == 0:
            gather_pass(0, TOK, tok)
        gather_end(c, TOK, tok)
        if c + 1 < chunks:
            gather_pass(c + 1, TOK, tok)

        @pl.loop(0, 2)
        def _(j):
            x = tok[c].reshape(8 * rows, -1)
            psend[c, j] = jnp.dot(x, enc_ref[:, columns((1 - core) * 2 + j)], preferred_element_type=F32)

        send(c, PAIR, psend.at[c], prec.at[c], pair_dev)

        @pl.loop(0, 2)
        def _(j):
            x = tok[c].reshape(8 * rows, -1)
            pown[c, j] = jnp.dot(x, enc_ref[:, columns(core * 2 + j)], preferred_element_type=F32)

    def pair_sum(c):
        arrive(c, PAIR, prec.at[c], pair_dev)
        xsend[c] = pown[c, 1 - xi] + prec[c, 1 - xi]
        send(c, XP, xsend.at[c], xrec.at[c], x_dev)

    def activate(c):
        arrive(c, XP, xrec.at[c], x_dev)
        total = pown[c, xi] + prec[c, xi] + xrec[c]
        mine = core * 2 + xi
        preact = enc_scale * total + bias_ref[mine]
        act[c, mine] = jnp.maximum(preact, 0.0).astype(BF16)
        send(c, XA, act.at[c, mine], act.at[c, mine], x_dev)
        send(c, CA, act.at[c, mine], act.at[c, mine], pair_dev)

    def pass_active(c):
        other = act.at[c, core * 2 + (1 - xi)]
        arrive(c, XA, other, x_dev)
        send(c, CB, other, other, pair_dev)

    def decode(c):
        arrive(c, CA, act.at[c, (1 - core) * 2 + xi], pair_dev)
        arrive(c, CB, act.at[c, (1 - core) * 2 + (1 - xi)], pair_dev)
        part = contract_columns(act[c, 0], dec_ref[:, 0:quarter])
        for q in range(1, 4):
            part = part + contract_columns(act[c, q], dec_ref[:, q * quarter:(q + 1) * quarter])
        part = (dec_scale * part).astype(BF16).reshape(8, rows, -1)
        for f in range(8):
            rpart[c, f % 2, f // 2] = part[f]
        send(c, YR, rpart.at[c, 1 - yi], yrec.at[c], y_dev)

    def fold_y(c):
        arrive(c, YR, yrec.at[c], y_dev)
        zsend[c] = (rpart[c, yi].astype(F32) + yrec[c].astype(F32)).astype(BF16)
        for step in (1, 2, 3):
            send(c, ZR + step - 1, zsend.at[c, z_at(step)], zrec.at[c, step - 1], z_dev(step))

    def fold_z(c):
        recon = rpart[c, yi, zi].astype(F32) + yrec[c, zi].astype(F32)
        for step in (1, 2, 3):
            arrive(c, ZR + step - 1, zrec.at[c, step - 1], z_dev(-step))
            recon = recon + zrec[c, step - 1].astype(F32)
        own = tok_ref[c * rows:(c + 1) * rows, :].astype(F32)
        err[c, feat] = (recon + dbias_ref[...] - own).astype(BF16)
        gather_begin(c, ERR, err)

    def pass_error(c):
        gather_pass(c, ERR, err)

    def grad(c):
        gather_end(c, ERR, err)

        @pl.loop(0, 2)
        def _(j):
            e = err[c].reshape(8 * rows, -1)
            g = jnp.dot(e, dec_ref[:, columns((1 - core) * 2 + j)], preferred_element_type=F32)
            gsend[c, j] = (dec_scale * g).astype(BF16)

        send(c, GP, gsend.at[c], grec.at[c], pair_dev)

        @pl.loop(0, 2)
        def _(j):
            e = err[c].reshape(8 * rows, -1)
            g = jnp.dot(e, dec_ref[:, columns(core * 2 + j)], preferred_element_type=F32)
            gown[c, j] = dec_scale * g

    def grad_pair(c):
        arrive(c, GP, grec.at[c], pair_dev)
        for j in range(2):
            both = gown[c, j] + grec[c, j].astype(F32)
            gown[c, j] = both
            xgsend[c, j] = both.astype(BF16)
        send(c, GX, xgsend.at[c], xgrec.at[c], x_dev)

    def mask(c):
        arrive(c, GX, xgrec.at[c], x_dev)
        for j in range(2):
            whole = gown[c, j] + xgrec[c, j].astype(F32)
            lit = act[c, core * 2 + j].astype(F32) > 0.0
            gp[c, core * 2 + j] = jnp.where(lit, whole, 0.0).astype(BF16)
        own = gp.at[c, pl.ds(core * 2, 2)]
        send(c, GM, own, own, pair_dev)

    for c in range(chunks):
        tok[c, feat] = tok_ref[c * rows:(c + 1) * rows, :]
        gather_begin(c, TOK, tok)
    stages = dict(partial=partial, pair_sum=pair_sum, activate=activate, pass_active=pass_active, decode=decode,
                  fold_y=fold_y, fold_z=fold_z, pass_error=pass_error, grad=grad, grad_pair=grad_pair, mask=mask)
    order = sorted((due + c * PERIOD, i, c, name) for i, (name, due) in enumerate(STAGES) for c in range(chunks))
    last_grad = max(i for i, item in enumerate(order) if item[3] == "grad_pair")
    for i, (_, _, c, name) in enumerate(order):
        stages[name](c)
        if i == last_grad:
            @pl.loop(0, 4)
            def _(q):
                left = err[...].reshape(chunks * 8 * rows, -1)
                right = jnp.concatenate([act[c, q] for c in range(chunks)], axis=0)
                dec_out[:, columns(q)] = (-LEARN_RATE * dec_scale * contract_rows(left, right)).astype(BF16)

    for c in range(chunks):
        arrive(c, GM, gp.at[c, pl.ds((1 - core) * 2, 2)], pair_dev)

    @pl.loop(0, 4)
    def _(q):
        left = tok[...].reshape(chunks * 8 * rows, -1)
        right = jnp.concatenate([gp[c, q] for c in range(chunks)], axis=0)
        enc_out[:, columns(q)] = (-LEARN_RATE * enc_scale * contract_rows(left, right)).astype(BF16)

    for moving in started:
        moving.wait_send()


def fused(layer_acts, enc_weight, dec_weight, enc_bias, dec_bias):
    tokens, width = layer_acts.shape[1:]
    features = enc_weight.shape[2]
    chunks, quarter = 4, features // 4
    rows = tokens // chunks
    enc_scale = (lax.axis_size("layer") * width) ** (-0.5)
    dec_scale = (features * lax.axis_size("feat")) ** (-0.5)
    whole = 8 * rows
    vmem = pl.BlockSpec(memory_space=pltpu.VMEM)
    half32 = pltpu.VMEM((chunks, 2, whole, quarter), F32)
    half16 = pltpu.VMEM((chunks, 2, whole, quarter), BF16)
    quarter32 = pltpu.VMEM((chunks, whole, quarter), F32)
    full16 = pltpu.VMEM((chunks, 4, whole, quarter), BF16)
    blocks = pltpu.VMEM((chunks, 8, rows, width), BF16)
    enc_step, dec_step = pl.pallas_call(
        functools.partial(kernel, chunks, rows, quarter, enc_scale, dec_scale),
        out_shape=[jax.ShapeDtypeStruct((width, features), BF16)] * 2,
        in_specs=[vmem] * 5,
        out_specs=[vmem] * 2,
        scratch_shapes=[
            blocks, half32, half32, half32, quarter32, quarter32, full16,
            pltpu.VMEM((chunks, 2, 4, rows, width), BF16),
            pltpu.VMEM((chunks, 4, rows, width), BF16),
            pltpu.VMEM((chunks, 4, rows, width), BF16),
            pltpu.VMEM((chunks, 3, rows, width), BF16),
            blocks, half16, half16, half32, half16, half16, full16,
            pltpu.SemaphoreType.DMA((chunks, 26)),
            pltpu.SemaphoreType.DMA((chunks, 26)),
        ],
        compiler_params=pltpu.CompilerParams(
            collective_id=0, has_side_effects=True, vmem_limit_bytes=58 * 2**20),
    )(layer_acts[0], enc_weight[0], jnp.swapaxes(dec_weight[0], 0, 1), enc_bias.reshape(4, 1, quarter), dec_bias)
    return enc_step[None], jnp.swapaxes(dec_step, 0, 1)[None]


def body(layer_acts, enc_weight, dec_weight, enc_bias, dec_bias):
    tok_local = layer_acts[0]
    enc_local = enc_weight[0]
    dec_local = dec_weight[0]
    model_width = enc_local.shape[0]
    slab_width = enc_local.shape[1]
    enc_scale = (layer_acts.shape[0] * lax.axis_size("layer") * model_width) ** (-0.5)
    dec_scale = (slab_width * lax.axis_size("feat")) ** (-0.5)
    whole_tokens = lax.all_gather(tok_local, "feat", axis=0, tiled=True)
    partial_value = jnp.dot(whole_tokens, enc_local, preferred_element_type=jnp.float32)
    preact = enc_scale * lax.psum(partial_value, "layer") + enc_bias
    active_b = jnp.maximum(preact, 0.0).astype(jnp.bfloat16)
    recon = lax.psum_scatter(
        dec_scale * jnp.dot(active_b, dec_local, preferred_element_type=jnp.float32),
        "feat",
        scatter_dimension=0,
        tiled=True,
    )
    error_b = (recon + dec_bias[0] - tok_local.astype(jnp.float32)).astype(jnp.bfloat16)
    whole_errors = lax.all_gather(error_b, "feat", axis=0, tiled=True)
    grad_dec = contract_rows(active_b, whole_errors)
    act_terms = dec_scale * contract_columns(whole_errors, dec_local)
    grad_act = lax.psum(act_terms, "layer")
    grad_pre = jnp.where(preact > 0.0, grad_act, 0.0).astype(jnp.bfloat16)
    grad_enc = contract_rows(whole_tokens, grad_pre)
    enc_step = (-LEARN_RATE * enc_scale * grad_enc).astype(jnp.bfloat16)[None]
    dec_step = (-LEARN_RATE * dec_scale * grad_dec).astype(jnp.bfloat16)[None]
    return (enc_step, dec_step)


def solution(mesh):
    in_specs = (
        P("layer", "feat", None),
        P("layer", None, "feat"),
        P("layer", "feat", None),
        P("feat"),
        P("layer", None),
    )
    out_specs = (P("layer", None, "feat"), P("layer", "feat", None))
    run = fused if (mesh.shape["layer"], mesh.shape["feat"]) == (4, 8) else body
    return jax.shard_map(run, mesh=mesh, in_specs=in_specs, out_specs=out_specs, check_vma=False)
```

```python
import functools

import jax
import jax.numpy as jnp
from jax import lax
from jax.experimental import pallas as pl
from jax.experimental.pallas import tpu as pltpu
from jax.sharding import PartitionSpec as P

LEARN_RATE = 4.0
MESH = pl.DeviceIdType.MESH
F32 = jnp.float32
BF16 = jnp.bfloat16

ORDER = (
    ("partial", 0), ("pair_sum", 0), ("partial", 1), ("pair_sum", 1),
    ("partial", 2), ("activate", 0), ("pair_sum", 2), ("activate", 1),
    ("pass_active", 0), ("partial", 3), ("decode", 0), ("activate", 2),
    ("pass_active", 1), ("pair_sum", 3), ("fold", 0), ("pass_active", 2),
    ("decode", 1), ("decode", 2), ("activate", 3), ("fold", 1),
    ("grad", 0), ("fold", 2), ("grad_pair", 0), ("pass_active", 3),
    ("grad", 1), ("decode", 3), ("grad_pair", 1), ("grad", 2),
    ("mask", 0), ("fold", 3), ("grad_pair", 2), ("grad", 3),
    ("grad_pair", 3), ("mask", 2), ("mask", 1), ("dec_all", 2),
    ("mask", 3),
)


def contract_rows(left, right):
    return lax.dot_general(left, right, (((0,), (0,)), ((), ())), preferred_element_type=F32)


def contract_columns(left, right):
    return lax.dot_general(left, right, (((1,), (1,)), ((), ())), preferred_element_type=F32)


def kernel(chunks, rows, quarter, enc_scale, dec_scale, tok_ref, enc_hbm, dec_hbm, bias_ref, dbias_ref,
           tok, gp, dec_out, enc_ref, dec_ref, dec_acc, psend, prec, pown, xsend, xrec, act, rpart, rrec, err,
           gsend, grec, gown, xgsend, xgrec, loads, sends, recvs):
    layer, feat = lax.axis_index("layer"), lax.axis_index("feat")
    xi, core = layer // 2, layer % 2
    pair_dev = (xi * 2 + (1 - core), feat)
    x_dev = ((1 - xi) * 2 + core, feat)
    steps = range(1, 8)

    load_enc = pltpu.make_async_copy(enc_hbm, enc_ref, loads.at[0])
    load_dec = pltpu.make_async_copy(dec_hbm, dec_ref, loads.at[1])
    load_enc.start()
    load_dec.start()

    def feat_at(step):
        return lax.rem(feat + step + 8, 8)

    def feat_dev(step):
        return (layer, feat_at(step))

    barrier = pltpu.get_barrier_semaphore()
    peers = [pair_dev, x_dev] + [feat_dev(step) for step in steps]
    for peer in peers:
        pl.semaphore_signal(barrier, inc=1, device_id=peer, device_id_type=MESH)
    for c in range(chunks):
        tok[c, feat] = tok_ref[c * rows:(c + 1) * rows, :]
    pl.semaphore_wait(barrier, len(peers))

    started = []

    def copy(c, kind, src, dst, dev):
        return pltpu.make_async_remote_copy(
            src_ref=src, dst_ref=dst, send_sem=sends.at[c, kind], recv_sem=recvs.at[c, kind],
            device_id=dev, device_id_type=MESH)

    def send(c, kind, src, dst, dev):
        moving = copy(c, kind, src, dst, dev)
        moving.start()
        started.append(moving)

    def arrive(c, kind, dst, dev):
        copy(c, kind, dst, dst, dev).wait_recv()

    def gather_begin(c, base, buf):
        own = buf.at[c, feat]
        for step in (4, 3, 5, 2, 6, 1, 7):
            send(c, base + step - 1, own, own, feat_dev(step))

    def gather_end(c, base, buf):
        for step in steps:
            arrive(c, base + step - 1, buf.at[c, feat_at(-step)], feat_dev(-step))

    TOK, ERR, RS, PAIR, XP, XA, CA, CB, GP, GX, GM = 0, 7, 14, 21, 23, 24, 25, 26, 27, 29, 31

    def columns(q):
        return pl.ds(pl.multiple_of(q * quarter, quarter), quarter)

    halves = ((0, 1 - xi), (1, xi))

    def partial(c):
        gather_end(c, TOK, tok)
        if c == 0:
            load_enc.wait()
        x = tok[c].reshape(8 * rows, -1)
        for i, j in halves:
            psend[c, i] = jnp.dot(x, enc_ref[:, columns((1 - core) * 2 + j)], preferred_element_type=F32)
            send(c, PAIR + i, psend.at[c, i], prec.at[c, i], pair_dev)
        for i, j in halves:
            pown[c, i] = jnp.dot(x, enc_ref[:, columns(core * 2 + j)], preferred_element_type=F32)

    def pair_sum(c):
        arrive(c, PAIR, prec.at[c, 0], pair_dev)
        xsend[c] = pown[c, 0] + prec[c, 0]
        send(c, XP, xsend.at[c], xrec.at[c], x_dev)

    def activate(c):
        arrive(c, PAIR + 1, prec.at[c, 1], pair_dev)
        arrive(c, XP, xrec.at[c], x_dev)
        total = pown[c, 1] + prec[c, 1] + xrec[c]
        mine = core * 2 + xi
        preact = enc_scale * total + bias_ref[mine]
        act[c, mine] = jnp.maximum(preact, 0.0).astype(BF16)
        send(c, XA, act.at[c, mine], act.at[c, mine], x_dev)
        send(c, CA, act.at[c, mine], act.at[c, mine], pair_dev)

    def pass_active(c):
        other = act.at[c, core * 2 + (1 - xi)]
        arrive(c, XA, other, x_dev)
        send(c, CB, other, other, pair_dev)

    def decode(c):
        if c == 0:
            load_dec.wait()
        arrive(c, CA, act.at[c, (1 - core) * 2 + xi], pair_dev)
        arrive(c, CB, act.at[c, (1 - core) * 2 + (1 - xi)], pair_dev)
        part = contract_columns(act[c, 0], dec_ref[:, 0:quarter])
        for q in range(1, 4):
            part = part + contract_columns(act[c, q], dec_ref[:, q * quarter:(q + 1) * quarter])
        rpart[c] = (dec_scale * part).astype(BF16).reshape(8, rows, -1)
        for step in (4, 3, 5, 2, 6, 1, 7):
            send(c, RS + step - 1, rpart.at[c, feat_at(step)], rrec.at[c, step - 1], feat_dev(step))

    def fold(c):
        recon = rpart[c, feat].astype(F32)
        for step in steps:
            arrive(c, RS + step - 1, rrec.at[c, step - 1], feat_dev(-step))
            recon = recon + rrec[c, step - 1].astype(F32)
        own = tok_ref[c * rows:(c + 1) * rows, :].astype(F32)
        err[c, feat] = (recon + dbias_ref[...] - own).astype(BF16)
        gather_begin(c, ERR, err)

    def grad(c):
        gather_end(c, ERR, err)
        e = err[c].reshape(8 * rows, -1)
        for j in range(2):
            g = jnp.dot(e, dec_ref[:, columns((1 - core) * 2 + j)], preferred_element_type=F32)
            gsend[c, j] = (dec_scale * g).astype(BF16)
            send(c, GP + j, gsend.at[c, j], grec.at[c, j], pair_dev)
        for j in range(2):
            g = jnp.dot(e, dec_ref[:, columns(core * 2 + j)], preferred_element_type=F32)
            gown[c, j] = dec_scale * g

    def grad_pair(c):
        for j in range(2):
            arrive(c, GP + j, grec.at[c, j], pair_dev)
            both = gown[c, j] + grec[c, j].astype(F32)
            gown[c, j] = both
            xgsend[c, j] = both.astype(BF16)
            send(c, GX + j, xgsend.at[c, j], xgrec.at[c, j], x_dev)

    def mask(c):
        for j in range(2):
            arrive(c, GX + j, xgrec.at[c, j], x_dev)
            whole = gown[c, j] + xgrec[c, j].astype(F32)
            q = core * 2 + j
            lit = act[c, q].astype(F32) > 0.0
            gp[c, q] = jnp.where(lit, whole, 0.0).astype(BF16)
            send(c, GM + j, gp.at[c, q], gp.at[c, q], pair_dev)

    store_dec = pltpu.make_async_copy(dec_acc, dec_out, loads.at[2])

    def dec_all(_):
        @pl.loop(0, 4)
        def _(q):
            left = err[...].reshape(chunks * 8 * rows, -1)
            right = jnp.concatenate([act[c, q] for c in range(chunks)], axis=0)
            dec_acc[:, columns(q)] = (-LEARN_RATE * dec_scale * contract_rows(left, right)).astype(BF16)

        store_dec.start()

    for c in range(chunks):
        gather_begin(c, TOK, tok)
    stages = dict(partial=partial, pair_sum=pair_sum, activate=activate, pass_active=pass_active, decode=decode,
                  fold=fold, grad=grad, grad_pair=grad_pair, mask=mask, dec_all=dec_all)
    for name, c in ORDER:
        stages[name](c)
    for c in range(chunks):
        for j in range(2):
            arrive(c, GM + j, gp.at[c, (1 - core) * 2 + j], pair_dev)
    store_dec.wait()
    for moving in started:
        moving.wait_send()


def finish(scale, tok_ref, gp_ref, dec_ref, enc_out, dec_out):
    chunks = tok_ref.shape[0]
    left = tok_ref[...].reshape(-1, tok_ref.shape[3])
    right = jnp.concatenate([gp_ref[c, 0] for c in range(chunks)], axis=0)
    enc_out[...] = (scale * contract_rows(left, right)).astype(BF16)
    dec_out[...] = dec_ref[...]


def fused(layer_acts, enc_weight, dec_weight, enc_bias, dec_bias):
    tokens, width = layer_acts.shape[1:]
    features = enc_weight.shape[2]
    chunks, quarter = 4, features // 4
    rows = tokens // chunks
    enc_scale = (lax.axis_size("layer") * width) ** (-0.5)
    dec_scale = (features * lax.axis_size("feat")) ** (-0.5)
    whole = 8 * rows
    vmem = pl.BlockSpec(memory_space=pltpu.VMEM)
    anywhere = pl.BlockSpec(memory_space=pl.ANY)
    half32 = pltpu.VMEM((chunks, 2, whole, quarter), F32)
    half16 = pltpu.VMEM((chunks, 2, whole, quarter), BF16)
    quarter32 = pltpu.VMEM((chunks, whole, quarter), F32)
    full16 = pltpu.VMEM((chunks, 4, whole, quarter), BF16)
    blocks = pltpu.VMEM((chunks, 8, rows, width), BF16)
    weights = pltpu.VMEM((width, features), BF16)
    step_shape = jax.ShapeDtypeStruct((width, features), BF16)
    tok, gp, dec_step = pl.pallas_call(
        functools.partial(kernel, chunks, rows, quarter, enc_scale, dec_scale),
        out_shape=[
            jax.ShapeDtypeStruct((chunks, 8, rows, width), BF16),
            jax.ShapeDtypeStruct((chunks, 4, whole, quarter), BF16),
            step_shape,
        ],
        in_specs=[vmem, anywhere, anywhere, vmem, vmem],
        out_specs=[vmem, vmem, anywhere],
        scratch_shapes=[
            weights, weights, weights, half32, half32, half32, quarter32, quarter32, full16, blocks,
            pltpu.VMEM((chunks, 7, rows, width), BF16),
            blocks, half16, half16, half32, half16, half16,
            pltpu.SemaphoreType.DMA((3,)),
            pltpu.SemaphoreType.DMA((chunks, 33)),
            pltpu.SemaphoreType.DMA((chunks, 33)),
        ],
        compiler_params=pltpu.CompilerParams(
            collective_id=0, has_side_effects=True, vmem_limit_bytes=56 * 2**20),
    )(layer_acts[0], enc_weight[0], jnp.swapaxes(dec_weight[0], 0, 1), enc_bias.reshape(4, 1, quarter), dec_bias)
    slab = pl.BlockSpec((width, quarter), lambda q: (0, q))
    enc_step, dec_step = pl.pallas_call(
        functools.partial(finish, -LEARN_RATE * enc_scale),
        out_shape=[step_shape, step_shape],
        grid=(4,),
        in_specs=[
            pl.BlockSpec((chunks, 8, rows, width), lambda q: (0, 0, 0, 0)),
            pl.BlockSpec((chunks, 1, whole, quarter), lambda q: (0, q, 0, 0)),
            slab,
        ],
        out_specs=[slab, slab],
        compiler_params=pltpu.CompilerParams(vmem_limit_bytes=60 * 2**20),
    )(tok, gp, dec_step)
    return enc_step[None], jnp.swapaxes(dec_step, 0, 1)[None]


def body(layer_acts, enc_weight, dec_weight, enc_bias, dec_bias):
    tok_local = layer_acts[0]
    enc_local = enc_weight[0]
    dec_local = dec_weight[0]
    model_width = enc_local.shape[0]
    slab_width = enc_local.shape[1]
    enc_scale = (layer_acts.shape[0] * lax.axis_size("layer") * model_width) ** (-0.5)
    dec_scale = (slab_width * lax.axis_size("feat")) ** (-0.5)
    whole_tokens = lax.all_gather(tok_local, "feat", axis=0, tiled=True)
    partial_value = jnp.dot(whole_tokens, enc_local, preferred_element_type=jnp.float32)
    preact = enc_scale * lax.psum(partial_value, "layer") + enc_bias
    active_b = jnp.maximum(preact, 0.0).astype(jnp.bfloat16)
    recon = lax.psum_scatter(
        dec_scale * jnp.dot(active_b, dec_local, preferred_element_type=jnp.float32),
        "feat",
        scatter_dimension=0,
        tiled=True,
    )
    error_b = (recon + dec_bias[0] - tok_local.astype(jnp.float32)).astype(jnp.bfloat16)
    whole_errors = lax.all_gather(error_b, "feat", axis=0, tiled=True)
    grad_dec = contract_rows(active_b, whole_errors)
    act_terms = dec_scale * contract_columns(whole_errors, dec_local)
    grad_act = lax.psum(act_terms, "layer")
    grad_pre = jnp.where(preact > 0.0, grad_act, 0.0).astype(jnp.bfloat16)
    grad_enc = contract_rows(whole_tokens, grad_pre)
    enc_step = (-LEARN_RATE * enc_scale * grad_enc).astype(jnp.bfloat16)[None]
    dec_step = (-LEARN_RATE * dec_scale * grad_dec).astype(jnp.bfloat16)[None]
    return (enc_step, dec_step)


def solution(mesh):
    in_specs = (
        P("layer", "feat", None),
        P("layer", None, "feat"),
        P("layer", "feat", None),
        P("feat"),
        P("layer", None),
    )
    out_specs = (P("layer", None, "feat"), P("layer", "feat", None))
    run = fused if (mesh.shape["layer"], mesh.shape["feat"]) == (4, 8) else body
    return jax.shard_map(run, mesh=mesh, in_specs=in_specs, out_specs=out_specs, check_vma=False)
```

```python
import functools

import jax
import jax.numpy as jnp
from jax import lax
from jax.experimental import pallas as pl
from jax.experimental.pallas import tpu as pltpu
from jax.sharding import PartitionSpec as P

LEARN_RATE = 4.0
MESH = pl.DeviceIdType.MESH
F32 = jnp.float32
BF16 = jnp.bfloat16

ORDER = (
    ("turn_dec", 0), ("partial", 0), ("turn_dec", 1), ("pair_sum", 0),
    ("partial", 1), ("pair_sum", 1), ("partial", 2), ("activate", 0),
    ("pair_sum", 2), ("activate", 1), ("pass_active", 0), ("partial", 3),
    ("decode", 0), ("activate", 2), ("pass_active", 1), ("pair_sum", 3),
    ("fold", 0), ("pass_active", 2), ("decode", 1), ("decode", 2),
    ("activate", 3), ("fold", 1), ("grad", 0), ("fold", 2),
    ("grad_pair", 0), ("pass_active", 3), ("grad", 1), ("decode", 3),
    ("grad_pair", 1), ("grad", 2), ("turn_tok", 0), ("mask", 0),
    ("fold", 3), ("grad_pair", 2), ("grad", 3), ("grad_pair", 3),
    ("mask", 2), ("mask", 1), ("dec_all", 2), ("keep", 0),
    ("keep", 1), ("keep", 2), ("mask", 3), ("keep", 3),
)


def contract_rows(left, right):
    return lax.dot_general(left, right, (((0,), (0,)), ((), ())), preferred_element_type=F32)


def contract_columns(left, right):
    return lax.dot_general(left, right, (((1,), (1,)), ((), ())), preferred_element_type=F32)


def kernel(chunks, rows, quarter, enc_scale, dec_scale, tok_ref, enc_hbm, dec_hbm, bias_ref, dbias_ref,
           tok_t, gp_out, dec_out, tok, gp, enc_ref, dec_ref, dec_flat, dec_acc, psend, prec, pown, xsend, xrec, act, rpart, rrec, err,
           gsend, grec, gown, xgsend, xgrec, loads, sends, recvs):
    layer, feat = lax.axis_index("layer"), lax.axis_index("feat")
    xi, core = layer // 2, layer % 2
    pair_dev = (xi * 2 + (1 - core), feat)
    x_dev = ((1 - xi) * 2 + core, feat)
    steps = range(1, 8)

    load_enc = pltpu.make_async_copy(enc_hbm, enc_ref, loads.at[0])
    load_dec = pltpu.make_async_copy(dec_hbm, dec_ref, loads.at[1])
    load_enc.start()
    load_dec.start()

    def feat_at(step):
        return lax.rem(feat + step + 8, 8)

    def feat_dev(step):
        return (layer, feat_at(step))

    barrier = pltpu.get_barrier_semaphore()
    peers = [pair_dev, x_dev] + [feat_dev(step) for step in steps]
    for peer in peers:
        pl.semaphore_signal(barrier, inc=1, device_id=peer, device_id_type=MESH)
    for c in range(chunks):
        tok[c, feat] = tok_ref[c * rows:(c + 1) * rows, :]
    pl.semaphore_wait(barrier, len(peers))

    started = []

    def copy(c, kind, src, dst, dev):
        return pltpu.make_async_remote_copy(
            src_ref=src, dst_ref=dst, send_sem=sends.at[c, kind], recv_sem=recvs.at[c, kind],
            device_id=dev, device_id_type=MESH)

    def send(c, kind, src, dst, dev):
        moving = copy(c, kind, src, dst, dev)
        moving.start()
        started.append(moving)

    def arrive(c, kind, dst, dev):
        copy(c, kind, dst, dst, dev).wait_recv()

    def gather_begin(c, base, buf):
        own = buf.at[c, feat]
        for step in (4, 3, 5, 2, 6, 1, 7):
            send(c, base + step - 1, own, own, feat_dev(step))

    def gather_end(c, base, buf):
        for step in steps:
            arrive(c, base + step - 1, buf.at[c, feat_at(-step)], feat_dev(-step))

    TOK, ERR, RS, PAIR, XP, XA, CA, CB, GP, GX, GM = 0, 7, 14, 21, 23, 24, 25, 26, 27, 29, 31

    def columns(q):
        return pl.ds(pl.multiple_of(q * quarter, quarter), quarter)

    halves = ((0, 1 - xi), (1, xi))

    def partial(c):
        gather_end(c, TOK, tok)
        if c == 0:
            load_enc.wait()
        x = tok[c].reshape(8 * rows, -1)
        for i, j in halves:
            psend[c, i] = jnp.dot(x, enc_ref[:, columns((1 - core) * 2 + j)], preferred_element_type=F32)
            send(c, PAIR + i, psend.at[c, i], prec.at[c, i], pair_dev)
        for i, j in halves:
            pown[c, i] = jnp.dot(x, enc_ref[:, columns(core * 2 + j)], preferred_element_type=F32)

    def pair_sum(c):
        arrive(c, PAIR, prec.at[c, 0], pair_dev)
        xsend[c] = pown[c, 0] + prec[c, 0]
        send(c, XP, xsend.at[c], xrec.at[c], x_dev)

    def activate(c):
        arrive(c, PAIR + 1, prec.at[c, 1], pair_dev)
        arrive(c, XP, xrec.at[c], x_dev)
        total = pown[c, 1] + prec[c, 1] + xrec[c]
        mine = core * 2 + xi
        preact = enc_scale * total + bias_ref[mine]
        act[c, mine] = jnp.maximum(preact, 0.0).astype(BF16)
        send(c, XA, act.at[c, mine], act.at[c, mine], x_dev)
        send(c, CA, act.at[c, mine], act.at[c, mine], pair_dev)

    def pass_active(c):
        other = act.at[c, core * 2 + (1 - xi)]
        arrive(c, XA, other, x_dev)
        send(c, CB, other, other, pair_dev)

    def decode(c):
        arrive(c, CA, act.at[c, (1 - core) * 2 + xi], pair_dev)
        arrive(c, CB, act.at[c, (1 - core) * 2 + (1 - xi)], pair_dev)
        part = jnp.dot(act[c, 0], dec_flat[0], preferred_element_type=F32)
        for q in range(1, 4):
            part = part + jnp.dot(act[c, q], dec_flat[q], preferred_element_type=F32)
        rpart[c] = (dec_scale * part).astype(BF16).reshape(8, rows, -1)
        for step in (4, 3, 5, 2, 6, 1, 7):
            send(c, RS + step - 1, rpart.at[c, feat_at(step)], rrec.at[c, step - 1], feat_dev(step))

    def fold(c):
        recon = rpart[c, feat].astype(F32)
        for step in steps:
            arrive(c, RS + step - 1, rrec.at[c, step - 1], feat_dev(-step))
            recon = recon + rrec[c, step - 1].astype(F32)
        own = tok_ref[c * rows:(c + 1) * rows, :].astype(F32)
        err[c, feat] = (recon + dbias_ref[...] - own).astype(BF16)
        gather_begin(c, ERR, err)

    def grad(c):
        gather_end(c, ERR, err)
        e = err[c].reshape(8 * rows, -1)
        for j in range(2):
            g = jnp.dot(e, dec_ref[:, columns((1 - core) * 2 + j)], preferred_element_type=F32)
            gsend[c, j] = (dec_scale * g).astype(BF16)
            send(c, GP + j, gsend.at[c, j], grec.at[c, j], pair_dev)
        for j in range(2):
            g = jnp.dot(e, dec_ref[:, columns(core * 2 + j)], preferred_element_type=F32)
            gown[c, j] = dec_scale * g

    def grad_pair(c):
        for j in range(2):
            arrive(c, GP + j, grec.at[c, j], pair_dev)
            both = gown[c, j] + grec[c, j].astype(F32)
            gown[c, j] = both
            xgsend[c, j] = both.astype(BF16)
            send(c, GX + j, xgsend.at[c, j], xgrec.at[c, j], x_dev)

    def mask(c):
        for j in range(2):
            arrive(c, GX + j, xgrec.at[c, j], x_dev)
            whole = gown[c, j] + xgrec[c, j].astype(F32)
            q = core * 2 + j
            lit = act[c, q].astype(F32) > 0.0
            gp[c, q] = jnp.where(lit, whole, 0.0).astype(BF16)
            send(c, GM + j, gp.at[c, q], gp.at[c, q], pair_dev)

    def turn_dec(half):
        if half == 0:
            load_dec.wait()
        for q in (2 * half, 2 * half + 1):
            dec_flat[q] = dec_ref[:, q * quarter:(q + 1) * quarter].T

    def turn_tok(_):
        tok_t[...] = tok[...].reshape(chunks * 8 * rows, -1).T

    store_gp = [
        [pltpu.make_async_copy(gp.at[c, pl.ds(h * 2, 2)], gp_out.at[c, pl.ds(h * 2, 2)], loads.at[3 + 2 * c + i])
         for i, h in enumerate((core, 1 - core))]
        for c in range(chunks)]

    def keep(c):
        for j in range(2):
            arrive(c, GM + j, gp.at[c, (1 - core) * 2 + j], pair_dev)
        store_gp[c][0].start()
        store_gp[c][1].start()

    store_dec = pltpu.make_async_copy(dec_acc, dec_out, loads.at[2])

    def dec_all(_):
        left = err[...].reshape(chunks * 8 * rows, -1).T
        for q in range(4):
            right = jnp.concatenate([act[c, q] for c in range(chunks)], axis=0)
            step = jnp.dot(left, right, preferred_element_type=F32)
            dec_acc[:, q * quarter:(q + 1) * quarter] = (-LEARN_RATE * dec_scale * step).astype(BF16)

        store_dec.start()

    for c in range(chunks):
        gather_begin(c, TOK, tok)
    stages = dict(partial=partial, pair_sum=pair_sum, activate=activate, pass_active=pass_active, decode=decode,
                  fold=fold, grad=grad, grad_pair=grad_pair, mask=mask, dec_all=dec_all,
                  turn_dec=turn_dec, turn_tok=turn_tok, keep=keep)
    for name, c in ORDER:
        stages[name](c)
    for c in range(chunks):
        for moving in store_gp[c]:
            moving.wait()
    store_dec.wait()
    for moving in started:
        moving.wait_send()


def finish(scale, tok_ref, gp_ref, dec_ref, enc_out, dec_out):
    right = jnp.concatenate([gp_ref[c, 0] for c in range(gp_ref.shape[0])], axis=0)
    enc_out[...] = (scale * jnp.dot(tok_ref[...], right, preferred_element_type=F32)).astype(BF16)
    dec_out[...] = dec_ref[...]


def fused(layer_acts, enc_weight, dec_weight, enc_bias, dec_bias):
    tokens, width = layer_acts.shape[1:]
    features = enc_weight.shape[2]
    chunks, quarter = 4, features // 4
    rows = tokens // chunks
    enc_scale = (lax.axis_size("layer") * width) ** (-0.5)
    dec_scale = (features * lax.axis_size("feat")) ** (-0.5)
    whole = 8 * rows
    vmem = pl.BlockSpec(memory_space=pltpu.VMEM)
    anywhere = pl.BlockSpec(memory_space=pl.ANY)
    half32 = pltpu.VMEM((chunks, 2, whole, quarter), F32)
    half16 = pltpu.VMEM((chunks, 2, whole, quarter), BF16)
    quarter32 = pltpu.VMEM((chunks, whole, quarter), F32)
    full16 = pltpu.VMEM((chunks, 4, whole, quarter), BF16)
    blocks = pltpu.VMEM((chunks, 8, rows, width), BF16)
    weights = pltpu.VMEM((width, features), BF16)
    step_shape = jax.ShapeDtypeStruct((width, features), BF16)
    tok_t, gp, dec_step = pl.pallas_call(
        functools.partial(kernel, chunks, rows, quarter, enc_scale, dec_scale),
        out_shape=[
            jax.ShapeDtypeStruct((width, tokens * 8), BF16),
            jax.ShapeDtypeStruct((chunks, 4, whole, quarter), BF16),
            step_shape,
        ],
        in_specs=[vmem, anywhere, anywhere, vmem, vmem],
        out_specs=[vmem, anywhere, anywhere],
        scratch_shapes=[
            blocks, full16, weights, weights, pltpu.VMEM((4, quarter, width), BF16), weights, half32, half32, half32, quarter32, quarter32, full16, blocks,
            pltpu.VMEM((chunks, 7, rows, width), BF16),
            blocks, half16, half16, half32, half16, half16,
            pltpu.SemaphoreType.DMA((3 + 2 * chunks,)),
            pltpu.SemaphoreType.DMA((chunks, 33)),
            pltpu.SemaphoreType.DMA((chunks, 33)),
        ],
        compiler_params=pltpu.CompilerParams(
            collective_id=0, has_side_effects=True, vmem_limit_bytes=56 * 2**20),
    )(layer_acts[0], enc_weight[0], jnp.swapaxes(dec_weight[0], 0, 1), enc_bias.reshape(4, 1, quarter), dec_bias)
    slab = pl.BlockSpec((width, quarter), lambda q: (0, q))
    enc_step, dec_step = pl.pallas_call(
        functools.partial(finish, -LEARN_RATE * enc_scale),
        out_shape=[step_shape, step_shape],
        grid=(4,),
        in_specs=[
            pl.BlockSpec((width, tokens * 8), lambda q: (0, 0)),
            pl.BlockSpec((chunks, 1, whole, quarter), lambda q: (0, q, 0, 0)),
            slab,
        ],
        out_specs=[slab, slab],
        compiler_params=pltpu.CompilerParams(vmem_limit_bytes=60 * 2**20),
    )(tok_t, gp, dec_step)
    return enc_step[None], jnp.swapaxes(dec_step, 0, 1)[None]


def body(layer_acts, enc_weight, dec_weight, enc_bias, dec_bias):
    tok_local = layer_acts[0]
    enc_local = enc_weight[0]
    dec_local = dec_weight[0]
    model_width = enc_local.shape[0]
    slab_width = enc_local.shape[1]
    enc_scale = (layer_acts.shape[0] * lax.axis_size("layer") * model_width) ** (-0.5)
    dec_scale = (slab_width * lax.axis_size("feat")) ** (-0.5)
    whole_tokens = lax.all_gather(tok_local, "feat", axis=0, tiled=True)
    partial_value = jnp.dot(whole_tokens, enc_local, preferred_element_type=jnp.float32)
    preact = enc_scale * lax.psum(partial_value, "layer") + enc_bias
    active_b = jnp.maximum(preact, 0.0).astype(jnp.bfloat16)
    recon = lax.psum_scatter(
        dec_scale * jnp.dot(active_b, dec_local, preferred_element_type=jnp.float32),
        "feat",
        scatter_dimension=0,
        tiled=True,
    )
    error_b = (recon + dec_bias[0] - tok_local.astype(jnp.float32)).astype(jnp.bfloat16)
    whole_errors = lax.all_gather(error_b, "feat", axis=0, tiled=True)
    grad_dec = contract_rows(active_b, whole_errors)
    act_terms = dec_scale * contract_columns(whole_errors, dec_local)
    grad_act = lax.psum(act_terms, "layer")
    grad_pre = jnp.where(preact > 0.0, grad_act, 0.0).astype(jnp.bfloat16)
    grad_enc = contract_rows(whole_tokens, grad_pre)
    enc_step = (-LEARN_RATE * enc_scale * grad_enc).astype(jnp.bfloat16)[None]
    dec_step = (-LEARN_RATE * dec_scale * grad_dec).astype(jnp.bfloat16)[None]
    return (enc_step, dec_step)


def solution(mesh):
    in_specs = (
        P("layer", "feat", None),
        P("layer", None, "feat"),
        P("layer", "feat", None),
        P("feat"),
        P("layer", None),
    )
    out_specs = (P("layer", None, "feat"), P("layer", "feat", None))
    run = fused if (mesh.shape["layer"], mesh.shape["feat"]) == (4, 8) else body
    return jax.shard_map(run, mesh=mesh, in_specs=in_specs, out_specs=out_specs, check_vma=False)
```

```python
import functools

import jax
import jax.numpy as jnp
from jax import lax
from jax.experimental import pallas as pl
from jax.experimental.pallas import tpu as pltpu
from jax.sharding import PartitionSpec as P

LEARN_RATE = 4.0
MESH = pl.DeviceIdType.MESH
F32 = jnp.float32
BF16 = jnp.bfloat16

ORDER = (
    ("turn_dec", 0), ("partial", 0), ("turn_dec", 1), ("pair_sum", 0),
    ("partial", 1), ("pair_sum", 1), ("partial", 2), ("activate", 0),
    ("pair_sum", 2), ("activate", 1), ("pass_active", 0), ("partial", 3),
    ("decode", 0), ("activate", 2), ("pass_active", 1), ("pair_sum", 3),
    ("fold", 0), ("pass_active", 2), ("decode", 1), ("decode", 2),
    ("activate", 3), ("fold", 1), ("grad", 0), ("fold", 2),
    ("grad_pair", 0), ("pass_active", 3), ("grad", 1), ("decode", 3),
    ("grad_pair", 1), ("grad", 2), ("turn_tok", 0), ("mask", 0),
    ("fold", 3), ("grad_pair", 2), ("grad", 3), ("grad_pair", 3),
    ("mask", 2), ("mask", 1), ("dec_all", 2), ("keep", 0),
    ("keep", 1), ("keep", 2), ("mask", 3), ("keep", 3),
)


def contract_rows(left, right):
    return lax.dot_general(left, right, (((0,), (0,)), ((), ())), preferred_element_type=F32)


def contract_columns(left, right):
    return lax.dot_general(left, right, (((1,), (1,)), ((), ())), preferred_element_type=F32)


def kernel(chunks, rows, quarter, enc_scale, dec_scale, tok_ref, enc_hbm, dec_hbm, bias_ref, dbias_ref,
           tok_t, gp, dec_acc, tok, enc_ref, dec_ref, dec_flat, psend, prec, pown, xsend, xrec, act, rpart, rrec, err,
           gsend, grec, gown, xgsend, xgrec, loads, sends, recvs):
    layer, feat = lax.axis_index("layer"), lax.axis_index("feat")
    xi, core = layer // 2, layer % 2
    pair_dev = (xi * 2 + (1 - core), feat)
    x_dev = ((1 - xi) * 2 + core, feat)
    steps = range(1, 8)

    load_enc = pltpu.make_async_copy(enc_hbm, enc_ref, loads.at[0])
    load_dec = pltpu.make_async_copy(dec_hbm, dec_ref, loads.at[1])
    load_enc.start()
    load_dec.start()

    def feat_at(step):
        return lax.rem(feat + step + 8, 8)

    def feat_dev(step):
        return (layer, feat_at(step))

    barrier = pltpu.get_barrier_semaphore()
    peers = [pair_dev, x_dev] + [feat_dev(step) for step in steps]
    for peer in peers:
        pl.semaphore_signal(barrier, inc=1, device_id=peer, device_id_type=MESH)
    for c in range(chunks):
        tok[c, feat] = tok_ref[c * rows:(c + 1) * rows, :]
    pl.semaphore_wait(barrier, len(peers))

    started = []

    def copy(c, kind, src, dst, dev):
        return pltpu.make_async_remote_copy(
            src_ref=src, dst_ref=dst, send_sem=sends.at[c, kind], recv_sem=recvs.at[c, kind],
            device_id=dev, device_id_type=MESH)

    def send(c, kind, src, dst, dev):
        moving = copy(c, kind, src, dst, dev)
        moving.start()
        started.append(moving)

    def arrive(c, kind, dst, dev):
        copy(c, kind, dst, dst, dev).wait_recv()

    def gather_begin(c, base, buf):
        own = buf.at[c, feat]
        for step in (4, 3, 5, 2, 6, 1, 7):
            send(c, base + step - 1, own, own, feat_dev(step))

    def gather_end(c, base, buf):
        for step in steps:
            arrive(c, base + step - 1, buf.at[c, feat_at(-step)], feat_dev(-step))

    TOK, ERR, RS, PAIR, XP, XA, CA, CB, GP, GX, GM = 0, 7, 14, 21, 23, 24, 25, 26, 27, 29, 31

    def columns(q):
        return pl.ds(pl.multiple_of(q * quarter, quarter), quarter)

    halves = ((0, 1 - xi), (1, xi))

    def partial(c):
        gather_end(c, TOK, tok)
        if c == 0:
            load_enc.wait()
        x = tok[c].reshape(8 * rows, -1)
        for i, j in halves:
            psend[c, i] = jnp.dot(x, enc_ref[:, columns((1 - core) * 2 + j)], preferred_element_type=F32)
            send(c, PAIR + i, psend.at[c, i], prec.at[c, i], pair_dev)
        for i, j in halves:
            pown[c, i] = jnp.dot(x, enc_ref[:, columns(core * 2 + j)], preferred_element_type=F32)

    def pair_sum(c):
        arrive(c, PAIR, prec.at[c, 0], pair_dev)
        xsend[c] = pown[c, 0] + prec[c, 0]
        send(c, XP, xsend.at[c], xrec.at[c], x_dev)

    def activate(c):
        arrive(c, PAIR + 1, prec.at[c, 1], pair_dev)
        arrive(c, XP, xrec.at[c], x_dev)
        total = pown[c, 1] + prec[c, 1] + xrec[c]
        mine = core * 2 + xi
        preact = enc_scale * total + bias_ref[mine]
        act[c, mine] = jnp.maximum(preact, 0.0).astype(BF16)
        send(c, XA, act.at[c, mine], act.at[c, mine], x_dev)
        send(c, CA, act.at[c, mine], act.at[c, mine], pair_dev)

    def pass_active(c):
        other = act.at[c, core * 2 + (1 - xi)]
        arrive(c, XA, other, x_dev)
        send(c, CB, other, other, pair_dev)

    def decode(c):
        arrive(c, CA, act.at[c, (1 - core) * 2 + xi], pair_dev)
        arrive(c, CB, act.at[c, (1 - core) * 2 + (1 - xi)], pair_dev)
        part = jnp.dot(act[c, 0], dec_flat[0], preferred_element_type=F32)
        for q in range(1, 4):
            part = part + jnp.dot(act[c, q], dec_flat[q], preferred_element_type=F32)
        rpart[c] = (dec_scale * part).astype(BF16).reshape(8, rows, -1)
        for step in (4, 3, 5, 2, 6, 1, 7):
            send(c, RS + step - 1, rpart.at[c, feat_at(step)], rrec.at[c, step - 1], feat_dev(step))

    def fold(c):
        recon = rpart[c, feat].astype(F32)
        for step in steps:
            arrive(c, RS + step - 1, rrec.at[c, step - 1], feat_dev(-step))
            recon = recon + rrec[c, step - 1].astype(F32)
        own = tok_ref[c * rows:(c + 1) * rows, :].astype(F32)
        err[c, feat] = (recon + dbias_ref[...] - own).astype(BF16)
        gather_begin(c, ERR, err)

    def grad(c):
        gather_end(c, ERR, err)
        e = err[c].reshape(8 * rows, -1)
        for j in range(2):
            g = jnp.dot(e, dec_ref[:, columns((1 - core) * 2 + j)], preferred_element_type=F32)
            gsend[c, j] = (dec_scale * g).astype(BF16)
            send(c, GP + j, gsend.at[c, j], grec.at[c, j], pair_dev)
        for j in range(2):
            g = jnp.dot(e, dec_ref[:, columns(core * 2 + j)], preferred_element_type=F32)
            gown[c, j] = dec_scale * g

    def grad_pair(c):
        for j in range(2):
            arrive(c, GP + j, grec.at[c, j], pair_dev)
            both = gown[c, j] + grec[c, j].astype(F32)
            gown[c, j] = both
            xgsend[c, j] = both.astype(BF16)
            send(c, GX + j, xgsend.at[c, j], xgrec.at[c, j], x_dev)

    def mask(c):
        for j in range(2):
            arrive(c, GX + j, xgrec.at[c, j], x_dev)
            whole = gown[c, j] + xgrec[c, j].astype(F32)
            q = core * 2 + j
            lit = act[c, q].astype(F32) > 0.0
            gp[c, q] = jnp.where(lit, whole, 0.0).astype(BF16)
            send(c, GM + j, gp.at[c, q], gp.at[c, q], pair_dev)

    def turn_dec(half):
        if half == 0:
            load_dec.wait()
        for q in (2 * half, 2 * half + 1):
            dec_flat[q] = dec_ref[:, q * quarter:(q + 1) * quarter].T

    def turn_tok(_):
        tok_t[...] = tok[...].reshape(chunks * 8 * rows, -1).T

    def keep(c):
        for j in range(2):
            arrive(c, GM + j, gp.at[c, (1 - core) * 2 + j], pair_dev)

    def dec_all(_):
        left = err[...].reshape(chunks * 8 * rows, -1).T
        for q in range(4):
            right = jnp.concatenate([act[c, q] for c in range(chunks)], axis=0)
            step = jnp.dot(left, right, preferred_element_type=F32)
            dec_acc[:, q * quarter:(q + 1) * quarter] = (-LEARN_RATE * dec_scale * step).astype(BF16)

    for c in range(chunks):
        gather_begin(c, TOK, tok)
    stages = dict(partial=partial, pair_sum=pair_sum, activate=activate, pass_active=pass_active, decode=decode,
                  fold=fold, grad=grad, grad_pair=grad_pair, mask=mask, dec_all=dec_all,
                  turn_dec=turn_dec, turn_tok=turn_tok, keep=keep)
    for name, c in ORDER:
        stages[name](c)
    for moving in started:
        moving.wait_send()


def finish(scale, tok_ref, gp_ref, dec_ref, enc_out, dec_out, slabs, sems):
    store_dec = pltpu.make_async_copy(dec_ref, dec_out, sems.at[0])
    store_dec.start()
    quarter = gp_ref.shape[3]
    stores = []
    for q in range(4):
        right = jnp.concatenate([gp_ref[c, q] for c in range(gp_ref.shape[0])], axis=0)
        slabs[q] = (scale * jnp.dot(tok_ref[...], right, preferred_element_type=F32)).astype(BF16)
        store = pltpu.make_async_copy(slabs.at[q], enc_out.at[:, q * quarter:(q + 1) * quarter], sems.at[1 + q])
        store.start()
        stores.append(store)
    for store in [store_dec] + stores:
        store.wait()


def fused(layer_acts, enc_weight, dec_weight, enc_bias, dec_bias):
    tokens, width = layer_acts.shape[1:]
    features = enc_weight.shape[2]
    chunks, quarter = 4, features // 4
    rows = tokens // chunks
    enc_scale = (lax.axis_size("layer") * width) ** (-0.5)
    dec_scale = (features * lax.axis_size("feat")) ** (-0.5)
    whole = 8 * rows
    vmem = pl.BlockSpec(memory_space=pltpu.VMEM)
    anywhere = pl.BlockSpec(memory_space=pl.ANY)
    half32 = pltpu.VMEM((chunks, 2, whole, quarter), F32)
    half16 = pltpu.VMEM((chunks, 2, whole, quarter), BF16)
    quarter32 = pltpu.VMEM((chunks, whole, quarter), F32)
    full16 = pltpu.VMEM((chunks, 4, whole, quarter), BF16)
    blocks = pltpu.VMEM((chunks, 8, rows, width), BF16)
    weights = pltpu.VMEM((width, features), BF16)
    step_shape = jax.ShapeDtypeStruct((width, features), BF16)
    tok_t, gp, dec_step = pl.pallas_call(
        functools.partial(kernel, chunks, rows, quarter, enc_scale, dec_scale),
        out_shape=[
            pltpu.VMEM((width, tokens * 8), BF16),
            full16,
            weights,
        ],
        in_specs=[vmem, anywhere, anywhere, vmem, vmem],
        out_specs=[vmem] * 3,
        scratch_shapes=[
            blocks, weights, weights, pltpu.VMEM((4, quarter, width), BF16), half32, half32, half32, quarter32, quarter32, full16, blocks,
            pltpu.VMEM((chunks, 7, rows, width), BF16),
            blocks, half16, half16, half32, half16, half16,
            pltpu.SemaphoreType.DMA((2,)),
            pltpu.SemaphoreType.DMA((chunks, 33)),
            pltpu.SemaphoreType.DMA((chunks, 33)),
        ],
        compiler_params=pltpu.CompilerParams(
            collective_id=0, has_side_effects=True, vmem_limit_bytes=56 * 2**20),
    )(layer_acts[0], enc_weight[0], jnp.swapaxes(dec_weight[0], 0, 1), enc_bias.reshape(4, 1, quarter), dec_bias)
    enc_step, dec_step = pl.pallas_call(
        functools.partial(finish, -LEARN_RATE * enc_scale),
        out_shape=[step_shape, step_shape],
        in_specs=[vmem] * 3,
        out_specs=[anywhere] * 2,
        scratch_shapes=[pltpu.VMEM((4, width, quarter), BF16), pltpu.SemaphoreType.DMA((5,))],
        compiler_params=pltpu.CompilerParams(vmem_limit_bytes=16 * 2**20),
    )(tok_t, gp, dec_step)
    return enc_step[None], jnp.swapaxes(dec_step, 0, 1)[None]


def body(layer_acts, enc_weight, dec_weight, enc_bias, dec_bias):
    tok_local = layer_acts[0]
    enc_local = enc_weight[0]
    dec_local = dec_weight[0]
    model_width = enc_local.shape[0]
    slab_width = enc_local.shape[1]
    enc_scale = (layer_acts.shape[0] * lax.axis_size("layer") * model_width) ** (-0.5)
    dec_scale = (slab_width * lax.axis_size("feat")) ** (-0.5)
    whole_tokens = lax.all_gather(tok_local, "feat", axis=0, tiled=True)
    partial_value = jnp.dot(whole_tokens, enc_local, preferred_element_type=jnp.float32)
    preact = enc_scale * lax.psum(partial_value, "layer") + enc_bias
    active_b = jnp.maximum(preact, 0.0).astype(jnp.bfloat16)
    recon = lax.psum_scatter(
        dec_scale * jnp.dot(active_b, dec_local, preferred_element_type=jnp.float32),
        "feat",
        scatter_dimension=0,
        tiled=True,
    )
    error_b = (recon + dec_bias[0] - tok_local.astype(jnp.float32)).astype(jnp.bfloat16)
    whole_errors = lax.all_gather(error_b, "feat", axis=0, tiled=True)
    grad_dec = contract_rows(active_b, whole_errors)
    act_terms = dec_scale * contract_columns(whole_errors, dec_local)
    grad_act = lax.psum(act_terms, "layer")
    grad_pre = jnp.where(preact > 0.0, grad_act, 0.0).astype(jnp.bfloat16)
    grad_enc = contract_rows(whole_tokens, grad_pre)
    enc_step = (-LEARN_RATE * enc_scale * grad_enc).astype(jnp.bfloat16)[None]
    dec_step = (-LEARN_RATE * dec_scale * grad_dec).astype(jnp.bfloat16)[None]
    return (enc_step, dec_step)


def solution(mesh):
    in_specs = (
        P("layer", "feat", None),
        P("layer", None, "feat"),
        P("layer", "feat", None),
        P("feat"),
        P("layer", None),
    )
    out_specs = (P("layer", None, "feat"), P("layer", "feat", None))
    run = fused if (mesh.shape["layer"], mesh.shape["feat"]) == (4, 8) else body
    return jax.shard_map(run, mesh=mesh, in_specs=in_specs, out_specs=out_specs, check_vma=False)
```

```python
import functools

import jax
import jax.numpy as jnp
from jax import lax
from jax.experimental import pallas as pl
from jax.experimental.pallas import tpu as pltpu
from jax.sharding import PartitionSpec as P

LEARN_RATE = 4.0
MESH = pl.DeviceIdType.MESH
F32 = jnp.float32
BF16 = jnp.bfloat16

ORDER = (
    ("turn_dec", 0), ("partial", 0), ("turn_dec", 1), ("pair_sum", 0),
    ("partial", 1), ("rest", 0), ("pair_sum", 1), ("rest", 1),
    ("activate", 0), ("partial", 2), ("activate", 1), ("pair_sum", 2),
    ("rest", 2), ("pass_active", 0), ("partial", 3), ("pass_active", 1),
    ("decode", 0), ("pair_sum", 3), ("decode", 1), ("rest", 3),
    ("fold", 0), ("activate", 3), ("activate", 2), ("pass_active", 3),
    ("fold", 1), ("grad", 0), ("pass_active", 2), ("decode", 3),
    ("decode", 2), ("grad_pair", 0), ("grad", 1), ("fold", 3),
    ("grad_pair", 1), ("fold", 2), ("grad", 3), ("grad_pair", 3),
    ("grad", 2), ("grad_pair", 2), ("turn_tok", 0), ("mask", 0),
    ("mask", 3), ("mask", 1), ("dec_all", 0), ("keep", 0),
    ("keep", 1), ("keep", 3), ("mask", 2), ("keep", 2),
)


def contract_rows(left, right):
    return lax.dot_general(left, right, (((0,), (0,)), ((), ())), preferred_element_type=F32)


def contract_columns(left, right):
    return lax.dot_general(left, right, (((1,), (1,)), ((), ())), preferred_element_type=F32)


def kernel(chunks, rows, quarter, enc_scale, dec_scale, tok_ref, enc_hbm, dec_hbm, bias_ref, dbias_ref,
           tok_t, gp, dec_acc, tok, tok_x, enc_ref, enc_x, dec_ref, dec_flat, psend, prec, pown, bsend, brec, bown, xsend, xrec, act, rpart, rrec, err,
           gsend, grec, gown, xgsend, xgrec, loads, sends, recvs):
    layer, feat = lax.axis_index("layer"), lax.axis_index("feat")
    xi, core = layer // 2, layer % 2
    pair_dev = (xi * 2 + (1 - core), feat)
    x_dev = ((1 - xi) * 2 + core, feat)
    steps = range(1, 8)
    ship = enc_x.shape[2]

    load_enc = pltpu.make_async_copy(enc_hbm, enc_ref, loads.at[0])
    load_dec = pltpu.make_async_copy(dec_hbm, dec_ref, loads.at[1])
    load_enc.start()
    load_dec.start()

    def feat_at(step):
        return lax.rem(feat + step + 8, 8)

    def feat_dev(step):
        return (layer, feat_at(step))

    barrier = pltpu.get_barrier_semaphore()
    peers = [pair_dev, x_dev] + [feat_dev(step) for step in steps]
    for peer in peers:
        pl.semaphore_signal(barrier, inc=1, device_id=peer, device_id_type=MESH)
    for c in range(chunks):
        tok[c, feat] = tok_ref[c * rows:(c + 1) * rows, :]
    pl.semaphore_wait(barrier, len(peers))

    started = []

    def copy(c, kind, src, dst, dev):
        return pltpu.make_async_remote_copy(
            src_ref=src, dst_ref=dst, send_sem=sends.at[c, kind], recv_sem=recvs.at[c, kind],
            device_id=dev, device_id_type=MESH)

    def send(c, kind, src, dst, dev):
        moving = copy(c, kind, src, dst, dev)
        moving.start()
        started.append(moving)

    def arrive(c, kind, dst, dev):
        copy(c, kind, dst, dst, dev).wait_recv()

    def gather_begin(c, base, buf):
        own = buf.at[c, feat]
        for step in (4, 3, 5, 2, 6, 1, 7):
            send(c, base + step - 1, own, own, feat_dev(step))

    def gather_end(c, base, buf):
        for step in steps:
            arrive(c, base + step - 1, buf.at[c, feat_at(-step)], feat_dev(-step))

    TOK, ERR, RS, PAIR, XP, XA, CA, CB, GP, GX, GM, TX, TOK_X, WX = 0, 7, 14, 21, 23, 24, 25, 26, 27, 29, 31, 33, 34, 41

    def columns(q, skip=0):
        return pl.ds(pl.multiple_of(q * quarter + skip, 128), quarter - skip)

    def partial(c):
        gather_end(c, TOK, tok)
        if c == 0:
            load_enc.wait()
        x = tok[c].reshape(8 * rows, -1)
        psend[c] = jnp.dot(x, enc_ref[:, columns((1 - core) * 2 + 1 - xi, ship)], preferred_element_type=F32)
        send(c, PAIR, psend.at[c], prec.at[c], pair_dev)
        pown[c] = jnp.dot(x, enc_ref[:, columns(core * 2 + 1 - xi, ship)], preferred_element_type=F32)

    def pair_sum(c):
        arrive(c, PAIR, prec.at[c], pair_dev)
        xsend[c] = pown[c] + prec[c]
        send(c, XP, xsend.at[c], xrec.at[c], x_dev)

    def rest(c):
        gather_end(c, TOK_X, tok_x)
        if c == 0:
            for h in range(2):
                arrive(0, WX + h, enc_x.at[h], x_dev)
        x = tok[c].reshape(8 * rows, -1)
        x_far = tok_x[c].reshape(8 * rows, -1)
        for h, dst in ((1 - core, bsend), (core, bown)):
            dst[c] = jnp.dot(x, enc_ref[:, columns(h * 2 + xi)], preferred_element_type=F32)
            dst[c, :, 0:ship] += jnp.dot(x_far, enc_x[h], preferred_element_type=F32)
            if dst is bsend:
                send(c, PAIR + 1, bsend.at[c], brec.at[c], pair_dev)

    def activate(c):
        arrive(c, PAIR + 1, brec.at[c], pair_dev)
        mine = core * 2 + xi
        bias = bias_ref[mine]
        near = bown[c] + brec[c]
        arrive(c, XP, xrec.at[c], x_dev)
        first = enc_scale * near[:, 0:ship] + bias[:, 0:ship]
        second = enc_scale * (near[:, ship:] + xrec[c]) + bias[:, ship:]
        act[c, mine, :, 0:ship] = jnp.maximum(first, 0.0).astype(BF16)
        act[c, mine, :, ship:quarter] = jnp.maximum(second, 0.0).astype(BF16)
        send(c, XA, act.at[c, mine], act.at[c, mine], x_dev)
        send(c, CA, act.at[c, mine], act.at[c, mine], pair_dev)

    def pass_active(c):
        other = act.at[c, core * 2 + (1 - xi)]
        arrive(c, XA, other, x_dev)
        send(c, CB, other, other, pair_dev)

    def decode(c):
        arrive(c, CA, act.at[c, (1 - core) * 2 + xi], pair_dev)
        arrive(c, CB, act.at[c, (1 - core) * 2 + (1 - xi)], pair_dev)
        part = jnp.dot(act[c, 0], dec_flat[0], preferred_element_type=F32)
        for q in range(1, 4):
            part = part + jnp.dot(act[c, q], dec_flat[q], preferred_element_type=F32)
        rpart[c] = (dec_scale * part).astype(BF16).reshape(8, rows, -1)
        for step in (4, 3, 5, 2, 6, 1, 7):
            send(c, RS + step - 1, rpart.at[c, feat_at(step)], rrec.at[c, step - 1], feat_dev(step))

    def fold(c):
        recon = rpart[c, feat].astype(F32)
        for step in steps:
            arrive(c, RS + step - 1, rrec.at[c, step - 1], feat_dev(-step))
            recon = recon + rrec[c, step - 1].astype(F32)
        own = tok_ref[c * rows:(c + 1) * rows, :].astype(F32)
        err[c, feat] = (recon + dbias_ref[...] - own).astype(BF16)
        gather_begin(c, ERR, err)

    def grad(c):
        gather_end(c, ERR, err)
        e = err[c].reshape(8 * rows, -1)
        for j in range(2):
            g = jnp.dot(e, dec_ref[:, columns((1 - core) * 2 + j)], preferred_element_type=F32)
            gsend[c, j] = (dec_scale * g).astype(BF16)
            send(c, GP + j, gsend.at[c, j], grec.at[c, j], pair_dev)
        for j in range(2):
            g = jnp.dot(e, dec_ref[:, columns(core * 2 + j)], preferred_element_type=F32)
            gown[c, j] = dec_scale * g

    def grad_pair(c):
        for j in range(2):
            arrive(c, GP + j, grec.at[c, j], pair_dev)
            both = gown[c, j] + grec[c, j].astype(F32)
            gown[c, j] = both
            xgsend[c, j] = both.astype(BF16)
            send(c, GX + j, xgsend.at[c, j], xgrec.at[c, j], x_dev)

    def mask(c):
        for j in range(2):
            arrive(c, GX + j, xgrec.at[c, j], x_dev)
            whole = gown[c, j] + xgrec[c, j].astype(F32)
            q = core * 2 + j
            lit = act[c, q].astype(F32) > 0.0
            gp[c, q] = jnp.where(lit, whole, 0.0).astype(BF16)
            send(c, GM + j, gp.at[c, q], gp.at[c, q], pair_dev)

    def turn_dec(half):
        if half == 0:
            load_dec.wait()
        for q in (2 * half, 2 * half + 1):
            dec_flat[q] = dec_ref[:, q * quarter:(q + 1) * quarter].T

    def turn_tok(_):
        tok_t[...] = tok[...].reshape(chunks * 8 * rows, -1).T

    def keep(c):
        for j in range(2):
            arrive(c, GM + j, gp.at[c, (1 - core) * 2 + j], pair_dev)

    def dec_all(_):
        left = err[...].reshape(chunks * 8 * rows, -1).T
        for q in range(4):
            right = jnp.concatenate([act[c, q] for c in range(chunks)], axis=0)
            step = jnp.dot(left, right, preferred_element_type=F32)
            dec_acc[:, q * quarter:(q + 1) * quarter] = (-LEARN_RATE * dec_scale * step).astype(BF16)

    def spread(c):
        arrive(c, TX, tok_x.at[c, feat], x_dev)
        gather_begin(c, TOK_X, tok_x)

    gather_begin(0, TOK, tok)
    for c in range(chunks):
        own = tok.at[c, feat]
        send(c, TX, own, tok_x.at[c, feat], x_dev)
    for h in range(2):
        sent = pl.ds(pl.multiple_of((h * 2 + 1 - xi) * quarter, quarter), ship)
        send(0, WX + h, enc_hbm.at[:, sent], enc_x.at[h], x_dev)
    gather_begin(1, TOK, tok)
    spread(0)
    spread(1)
    for c in range(2, chunks):
        gather_begin(c, TOK, tok)
        spread(c)
    stages = dict(partial=partial, pair_sum=pair_sum, activate=activate, pass_active=pass_active, decode=decode,
                  fold=fold, grad=grad, grad_pair=grad_pair, mask=mask, dec_all=dec_all, rest=rest,
                  turn_dec=turn_dec, turn_tok=turn_tok, keep=keep)
    for name, c in ORDER:
        stages[name](c)
    for moving in started:
        moving.wait_send()


def finish(scale, tok_ref, gp_ref, dec_ref, enc_out, dec_out, slabs, sems):
    store_dec = pltpu.make_async_copy(dec_ref, dec_out, sems.at[0])
    store_dec.start()
    quarter = gp_ref.shape[3]
    stores = []
    for q in range(4):
        right = jnp.concatenate([gp_ref[c, q] for c in range(gp_ref.shape[0])], axis=0)
        slabs[q] = (scale * jnp.dot(tok_ref[...], right, preferred_element_type=F32)).astype(BF16)
        store = pltpu.make_async_copy(slabs.at[q], enc_out.at[:, q * quarter:(q + 1) * quarter], sems.at[1 + q])
        store.start()
        stores.append(store)
    for store in [store_dec] + stores:
        store.wait()


def fused(layer_acts, enc_weight, dec_weight, enc_bias, dec_bias):
    tokens, width = layer_acts.shape[1:]
    features = enc_weight.shape[2]
    chunks, quarter = 4, features // 4
    rows = tokens // chunks
    enc_scale = (lax.axis_size("layer") * width) ** (-0.5)
    dec_scale = (features * lax.axis_size("feat")) ** (-0.5)
    whole = 8 * rows
    vmem = pl.BlockSpec(memory_space=pltpu.VMEM)
    anywhere = pl.BlockSpec(memory_space=pl.ANY)
    half32 = pltpu.VMEM((chunks, 2, whole, quarter), F32)
    half16 = pltpu.VMEM((chunks, 2, whole, quarter), BF16)
    ship = quarter // 4
    quarter32 = pltpu.VMEM((chunks, whole, quarter), F32)
    short32 = pltpu.VMEM((chunks, whole, quarter - ship), F32)
    full16 = pltpu.VMEM((chunks, 4, whole, quarter), BF16)
    blocks = pltpu.VMEM((chunks, 8, rows, width), BF16)
    weights = pltpu.VMEM((width, features), BF16)
    step_shape = jax.ShapeDtypeStruct((width, features), BF16)
    tok_t, gp, dec_step = pl.pallas_call(
        functools.partial(kernel, chunks, rows, quarter, enc_scale, dec_scale),
        out_shape=[
            pltpu.VMEM((width, tokens * 8), BF16),
            full16,
            weights,
        ],
        in_specs=[vmem, anywhere, anywhere, vmem, vmem],
        out_specs=[vmem] * 3,
        scratch_shapes=[
            blocks, blocks, weights, pltpu.VMEM((2, width, ship), BF16), weights,
            pltpu.VMEM((4, quarter, width), BF16), short32, short32, short32, quarter32, quarter32, quarter32,
            short32, short32, full16, blocks,
            pltpu.VMEM((chunks, 7, rows, width), BF16),
            blocks, half16, half16, half32, half16, half16,
            pltpu.SemaphoreType.DMA((2,)),
            pltpu.SemaphoreType.DMA((chunks, 43)),
            pltpu.SemaphoreType.DMA((chunks, 43)),
        ],
        compiler_params=pltpu.CompilerParams(
            collective_id=0, has_side_effects=True, vmem_limit_bytes=56 * 2**20),
    )(layer_acts[0], enc_weight[0], jnp.swapaxes(dec_weight[0], 0, 1), enc_bias.reshape(4, 1, quarter), dec_bias)
    enc_step, dec_step = pl.pallas_call(
        functools.partial(finish, -LEARN_RATE * enc_scale),
        out_shape=[step_shape, step_shape],
        in_specs=[vmem] * 3,
        out_specs=[anywhere] * 2,
        scratch_shapes=[pltpu.VMEM((4, width, quarter), BF16), pltpu.SemaphoreType.DMA((5,))],
        compiler_params=pltpu.CompilerParams(vmem_limit_bytes=16 * 2**20),
    )(tok_t, gp, dec_step)
    return enc_step[None], jnp.swapaxes(dec_step, 0, 1)[None]


def body(layer_acts, enc_weight, dec_weight, enc_bias, dec_bias):
    tok_local = layer_acts[0]
    enc_local = enc_weight[0]
    dec_local = dec_weight[0]
    model_width = enc_local.shape[0]
    slab_width = enc_local.shape[1]
    enc_scale = (layer_acts.shape[0] * lax.axis_size("layer") * model_width) ** (-0.5)
    dec_scale = (slab_width * lax.axis_size("feat")) ** (-0.5)
    whole_tokens = lax.all_gather(tok_local, "feat", axis=0, tiled=True)
    partial_value = jnp.dot(whole_tokens, enc_local, preferred_element_type=jnp.float32)
    preact = enc_scale * lax.psum(partial_value, "layer") + enc_bias
    active_b = jnp.maximum(preact, 0.0).astype(jnp.bfloat16)
    recon = lax.psum_scatter(
        dec_scale * jnp.dot(active_b, dec_local, preferred_element_type=jnp.float32),
        "feat",
        scatter_dimension=0,
        tiled=True,
    )
    error_b = (recon + dec_bias[0] - tok_local.astype(jnp.float32)).astype(jnp.bfloat16)
    whole_errors = lax.all_gather(error_b, "feat", axis=0, tiled=True)
    grad_dec = contract_rows(active_b, whole_errors)
    act_terms = dec_scale * contract_columns(whole_errors, dec_local)
    grad_act = lax.psum(act_terms, "layer")
    grad_pre = jnp.where(preact > 0.0, grad_act, 0.0).astype(jnp.bfloat16)
    grad_enc = contract_rows(whole_tokens, grad_pre)
    enc_step = (-LEARN_RATE * enc_scale * grad_enc).astype(jnp.bfloat16)[None]
    dec_step = (-LEARN_RATE * dec_scale * grad_dec).astype(jnp.bfloat16)[None]
    return (enc_step, dec_step)


def solution(mesh):
    in_specs = (
        P("layer", "feat", None),
        P("layer", None, "feat"),
        P("layer", "feat", None),
        P("feat"),
        P("layer", None),
    )
    out_specs = (P("layer", None, "feat"), P("layer", "feat", None))
    run = fused if (mesh.shape["layer"], mesh.shape["feat"]) == (4, 8) else body
    return jax.shard_map(run, mesh=mesh, in_specs=in_specs, out_specs=out_specs, check_vma=False)
```

```python
import functools

import jax
import jax.numpy as jnp
from jax import lax
from jax.experimental import pallas as pl
from jax.experimental.pallas import tpu as pltpu
from jax.sharding import PartitionSpec as P

LEARN_RATE = 4.0
MESH = pl.DeviceIdType.MESH
F32 = jnp.float32
BF16 = jnp.bfloat16

ORDER = (
    ("turn_dec", 0), ("partial", 0), ("turn_dec", 1), ("pair_sum", 0),
    ("partial", 1), ("pair_sum", 1), ("activate", 0), ("partial", 2),
    ("pair_sum", 2), ("partial", 3), ("pass_active", 0), ("activate", 1),
    ("decode", 0), ("activate", 2), ("pass_active", 1), ("pair_sum", 3),
    ("fold", 0), ("decode", 1), ("pass_active", 2), ("pass_error", 0),
    ("decode", 2), ("activate", 3), ("fold", 1), ("grad", 0),
    ("grad_pair", 0), ("fold", 2), ("pass_active", 3), ("pass_error", 1),
    ("decode", 3), ("grad", 1), ("pass_error", 2), ("grad_pair", 1),
    ("fold", 3), ("grad", 2), ("pass_error", 3), ("grad_pair", 2),
    ("grad", 3), ("mask", 1), ("grad_pair", 3), ("turn_tok", 0),
    ("mask", 0), ("mask", 2), ("dec_all", 0), ("keep", 0),
    ("keep", 1), ("keep", 2), ("mask", 3), ("keep", 3),
)


def contract_rows(left, right):
    return lax.dot_general(left, right, (((0,), (0,)), ((), ())), preferred_element_type=F32)


def contract_columns(left, right):
    return lax.dot_general(left, right, (((1,), (1,)), ((), ())), preferred_element_type=F32)


def kernel(chunks, rows, quarter, enc_scale, dec_scale, tok_ref, enc_hbm, dec_hbm, bias_ref, dbias_ref,
           tok_t, gp, dec_acc, tok, enc_ref, dec_ref, dec_flat, psend, prec, pown, xsend, xrec, act, rpart, rrec, err,
           gsend, grec, gown, xgsend, xgrec, loads, sends, recvs):
    layer, feat = lax.axis_index("layer"), lax.axis_index("feat")
    xi, core = layer // 2, layer % 2
    pair_dev = (xi * 2 + (1 - core), feat)
    x_dev = ((1 - xi) * 2 + core, feat)
    steps = range(1, 8)
    y_feat = (feat // 2) * 2 + (1 - feat % 2)
    y_dev = (layer, y_feat)

    load_enc = pltpu.make_async_copy(enc_hbm, enc_ref, loads.at[0])
    load_dec = pltpu.make_async_copy(dec_hbm, dec_ref, loads.at[1])
    load_enc.start()
    load_dec.start()

    def feat_at(step):
        return lax.rem(feat + step + 8, 8)

    def feat_dev(step):
        return (layer, feat_at(step))

    barrier = pltpu.get_barrier_semaphore()
    peers = [pair_dev, x_dev] + [feat_dev(step) for step in steps]
    for peer in peers:
        pl.semaphore_signal(barrier, inc=1, device_id=peer, device_id_type=MESH)
    for c in range(chunks):
        tok[c, feat] = tok_ref[c * rows:(c + 1) * rows, :]
    pl.semaphore_wait(barrier, len(peers))

    started = []

    def copy(c, kind, src, dst, dev):
        return pltpu.make_async_remote_copy(
            src_ref=src, dst_ref=dst, send_sem=sends.at[c, kind], recv_sem=recvs.at[c, kind],
            device_id=dev, device_id_type=MESH)

    def send(c, kind, src, dst, dev):
        moving = copy(c, kind, src, dst, dev)
        moving.start()
        started.append(moving)

    def arrive(c, kind, dst, dev):
        copy(c, kind, dst, dst, dev).wait_recv()

    def gather_begin(c, base, buf):
        own = buf.at[c, feat]
        for step in (4, 3, 5, 2, 6, 1, 7):
            send(c, base + step - 1, own, own, feat_dev(step))

    def gather_end(c, base, buf):
        for step in steps:
            arrive(c, base + step - 1, buf.at[c, feat_at(-step)], feat_dev(-step))

    def staged_begin(c, base, buf):
        own = buf.at[c, feat]
        for step in (4, 2, 6):
            send(c, base + step - 1, own, own, feat_dev(step))
        send(c, base, own, own, y_dev)

    def staged_pass(c, base, buf):
        for step in (2, 6, 4):
            slot = buf.at[c, feat_at(-step)]
            arrive(c, base + step - 1, slot, feat_dev(-step))
            send(c, base + step, slot, slot, y_dev)

    def staged_end(c, base, buf):
        arrive(c, base, buf.at[c, y_feat], y_dev)
        for step in (2, 6, 4):
            arrive(c, base + step, buf.at[c, lax.rem(y_feat - step + 8, 8)], y_dev)

    def pass_error(c):
        staged_pass(c, ERR, err)

    TOK, ERR, RS, PAIR, XP, XA, CA, CB, GP, GX, GM = 0, 7, 14, 21, 23, 24, 25, 26, 27, 29, 31

    def columns(q):
        return pl.ds(pl.multiple_of(q * quarter, quarter), quarter)

    halves = ((0, 1 - xi), (1, xi))

    def partial(c):
        gather_end(c, TOK, tok)
        if c == 0:
            load_enc.wait()
        x = tok[c].reshape(8 * rows, -1)
        for i, j in halves:
            psend[c, i] = jnp.dot(x, enc_ref[:, columns((1 - core) * 2 + j)], preferred_element_type=F32)
            send(c, PAIR + i, psend.at[c, i], prec.at[c, i], pair_dev)
        for i, j in halves:
            pown[c, i] = jnp.dot(x, enc_ref[:, columns(core * 2 + j)], preferred_element_type=F32)

    def pair_sum(c):
        arrive(c, PAIR, prec.at[c, 0], pair_dev)
        xsend[c] = pown[c, 0] + prec[c, 0]
        send(c, XP, xsend.at[c], xrec.at[c], x_dev)

    def activate(c):
        arrive(c, PAIR + 1, prec.at[c, 1], pair_dev)
        arrive(c, XP, xrec.at[c], x_dev)
        total = pown[c, 1] + prec[c, 1] + xrec[c]
        mine = core * 2 + xi
        preact = enc_scale * total + bias_ref[mine]
        act[c, mine] = jnp.maximum(preact, 0.0).astype(BF16)
        send(c, XA, act.at[c, mine], act.at[c, mine], x_dev)
        send(c, CA, act.at[c, mine], act.at[c, mine], pair_dev)

    def pass_active(c):
        other = act.at[c, core * 2 + (1 - xi)]
        arrive(c, XA, other, x_dev)
        send(c, CB, other, other, pair_dev)

    def decode(c):
        arrive(c, CA, act.at[c, (1 - core) * 2 + xi], pair_dev)
        arrive(c, CB, act.at[c, (1 - core) * 2 + (1 - xi)], pair_dev)
        part = jnp.dot(act[c, 0], dec_flat[0], preferred_element_type=F32)
        for q in range(1, 4):
            part = part + jnp.dot(act[c, q], dec_flat[q], preferred_element_type=F32)
        rpart[c] = (dec_scale * part).astype(BF16).reshape(8, rows, -1)
        for step in (4, 3, 5, 2, 6, 1, 7):
            send(c, RS + step - 1, rpart.at[c, feat_at(step)], rrec.at[c, step - 1], feat_dev(step))

    def fold(c):
        recon = rpart[c, feat].astype(F32)
        for step in steps:
            arrive(c, RS + step - 1, rrec.at[c, step - 1], feat_dev(-step))
            recon = recon + rrec[c, step - 1].astype(F32)
        own = tok_ref[c * rows:(c + 1) * rows, :].astype(F32)
        err[c, feat] = (recon + dbias_ref[...] - own).astype(BF16)
        staged_begin(c, ERR, err)

    def grad(c):
        staged_end(c, ERR, err)
        e = err[c].reshape(8 * rows, -1)
        for j in range(2):
            g = jnp.dot(e, dec_ref[:, columns((1 - core) * 2 + j)], preferred_element_type=F32)
            gsend[c, j] = (dec_scale * g).astype(BF16)
            send(c, GP + j, gsend.at[c, j], grec.at[c, j], pair_dev)
        for j in range(2):
            g = jnp.dot(e, dec_ref[:, columns(core * 2 + j)], preferred_element_type=F32)
            gown[c, j] = dec_scale * g

    def grad_pair(c):
        for j in range(2):
            arrive(c, GP + j, grec.at[c, j], pair_dev)
            both = gown[c, j] + grec[c, j].astype(F32)
            gown[c, j] = both
            xgsend[c, j] = both.astype(BF16)
            send(c, GX + j, xgsend.at[c, j], xgrec.at[c, j], x_dev)

    def mask(c):
        for j in range(2):
            arrive(c, GX + j, xgrec.at[c, j], x_dev)
            whole = gown[c, j] + xgrec[c, j].astype(F32)
            q = core * 2 + j
            lit = act[c, q].astype(F32) > 0.0
            gp[c, q] = jnp.where(lit, whole, 0.0).astype(BF16)
            send(c, GM + j, gp.at[c, q], gp.at[c, q], pair_dev)

    def turn_dec(half):
        if half == 0:
            load_dec.wait()
        for q in (2 * half, 2 * half + 1):
            dec_flat[q] = dec_ref[:, q * quarter:(q + 1) * quarter].T

    def turn_tok(_):
        tok_t[...] = tok[...].reshape(chunks * 8 * rows, -1).T

    def keep(c):
        for j in range(2):
            arrive(c, GM + j, gp.at[c, (1 - core) * 2 + j], pair_dev)

    def dec_all(_):
        left = err[...].reshape(chunks * 8 * rows, -1).T
        for q in range(4):
            right = jnp.concatenate([act[c, q] for c in range(chunks)], axis=0)
            step = jnp.dot(left, right, preferred_element_type=F32)
            dec_acc[:, q * quarter:(q + 1) * quarter] = (-LEARN_RATE * dec_scale * step).astype(BF16)

    for c in range(chunks):
        gather_begin(c, TOK, tok)
    stages = dict(partial=partial, pair_sum=pair_sum, activate=activate, pass_active=pass_active, decode=decode,
                  fold=fold, grad=grad, grad_pair=grad_pair, mask=mask, dec_all=dec_all, pass_error=pass_error,
                  turn_dec=turn_dec, turn_tok=turn_tok, keep=keep)
    for name, c in ORDER:
        stages[name](c)
    for moving in started:
        moving.wait_send()


def finish(scale, tok_ref, gp_ref, dec_ref, enc_out, dec_out, slabs, sems):
    store_dec = pltpu.make_async_copy(dec_ref, dec_out, sems.at[0])
    store_dec.start()
    quarter = gp_ref.shape[3]
    stores = []
    for q in range(4):
        right = jnp.concatenate([gp_ref[c, q] for c in range(gp_ref.shape[0])], axis=0)
        slabs[q] = (scale * jnp.dot(tok_ref[...], right, preferred_element_type=F32)).astype(BF16)
        store = pltpu.make_async_copy(slabs.at[q], enc_out.at[:, q * quarter:(q + 1) * quarter], sems.at[1 + q])
        store.start()
        stores.append(store)
    for store in [store_dec] + stores:
        store.wait()


def fused(layer_acts, enc_weight, dec_weight, enc_bias, dec_bias):
    tokens, width = layer_acts.shape[1:]
    features = enc_weight.shape[2]
    chunks, quarter = 4, features // 4
    rows = tokens // chunks
    enc_scale = (lax.axis_size("layer") * width) ** (-0.5)
    dec_scale = (features * lax.axis_size("feat")) ** (-0.5)
    whole = 8 * rows
    vmem = pl.BlockSpec(memory_space=pltpu.VMEM)
    anywhere = pl.BlockSpec(memory_space=pl.ANY)
    half32 = pltpu.VMEM((chunks, 2, whole, quarter), F32)
    half16 = pltpu.VMEM((chunks, 2, whole, quarter), BF16)
    quarter32 = pltpu.VMEM((chunks, whole, quarter), F32)
    full16 = pltpu.VMEM((chunks, 4, whole, quarter), BF16)
    blocks = pltpu.VMEM((chunks, 8, rows, width), BF16)
    weights = pltpu.VMEM((width, features), BF16)
    step_shape = jax.ShapeDtypeStruct((width, features), BF16)
    tok_t, gp, dec_step = pl.pallas_call(
        functools.partial(kernel, chunks, rows, quarter, enc_scale, dec_scale),
        out_shape=[
            pltpu.VMEM((width, tokens * 8), BF16),
            full16,
            weights,
        ],
        in_specs=[vmem, anywhere, anywhere, vmem, vmem],
        out_specs=[vmem] * 3,
        scratch_shapes=[
            blocks, weights, weights, pltpu.VMEM((4, quarter, width), BF16), half32, half32, half32, quarter32, quarter32, full16, blocks,
            pltpu.VMEM((chunks, 7, rows, width), BF16),
            blocks, half16, half16, half32, half16, half16,
            pltpu.SemaphoreType.DMA((2,)),
            pltpu.SemaphoreType.DMA((chunks, 33)),
            pltpu.SemaphoreType.DMA((chunks, 33)),
        ],
        compiler_params=pltpu.CompilerParams(
            collective_id=0, has_side_effects=True, vmem_limit_bytes=56 * 2**20),
    )(layer_acts[0], enc_weight[0], jnp.swapaxes(dec_weight[0], 0, 1), enc_bias.reshape(4, 1, quarter), dec_bias)
    enc_step, dec_step = pl.pallas_call(
        functools.partial(finish, -LEARN_RATE * enc_scale),
        out_shape=[step_shape, step_shape],
        in_specs=[vmem] * 3,
        out_specs=[anywhere] * 2,
        scratch_shapes=[pltpu.VMEM((4, width, quarter), BF16), pltpu.SemaphoreType.DMA((5,))],
        compiler_params=pltpu.CompilerParams(vmem_limit_bytes=16 * 2**20),
    )(tok_t, gp, dec_step)
    return enc_step[None], jnp.swapaxes(dec_step, 0, 1)[None]


def body(layer_acts, enc_weight, dec_weight, enc_bias, dec_bias):
    tok_local = layer_acts[0]
    enc_local = enc_weight[0]
    dec_local = dec_weight[0]
    model_width = enc_local.shape[0]
    slab_width = enc_local.shape[1]
    enc_scale = (layer_acts.shape[0] * lax.axis_size("layer") * model_width) ** (-0.5)
    dec_scale = (slab_width * lax.axis_size("feat")) ** (-0.5)
    whole_tokens = lax.all_gather(tok_local, "feat", axis=0, tiled=True)
    partial_value = jnp.dot(whole_tokens, enc_local, preferred_element_type=jnp.float32)
    preact = enc_scale * lax.psum(partial_value, "layer") + enc_bias
    active_b = jnp.maximum(preact, 0.0).astype(jnp.bfloat16)
    recon = lax.psum_scatter(
        dec_scale * jnp.dot(active_b, dec_local, preferred_element_type=jnp.float32),
        "feat",
        scatter_dimension=0,
        tiled=True,
    )
    error_b = (recon + dec_bias[0] - tok_local.astype(jnp.float32)).astype(jnp.bfloat16)
    whole_errors = lax.all_gather(error_b, "feat", axis=0, tiled=True)
    grad_dec = contract_rows(active_b, whole_errors)
    act_terms = dec_scale * contract_columns(whole_errors, dec_local)
    grad_act = lax.psum(act_terms, "layer")
    grad_pre = jnp.where(preact > 0.0, grad_act, 0.0).astype(jnp.bfloat16)
    grad_enc = contract_rows(whole_tokens, grad_pre)
    enc_step = (-LEARN_RATE * enc_scale * grad_enc).astype(jnp.bfloat16)[None]
    dec_step = (-LEARN_RATE * dec_scale * grad_dec).astype(jnp.bfloat16)[None]
    return (enc_step, dec_step)


def solution(mesh):
    in_specs = (
        P("layer", "feat", None),
        P("layer", None, "feat"),
        P("layer", "feat", None),
        P("feat"),
        P("layer", None),
    )
    out_specs = (P("layer", None, "feat"), P("layer", "feat", None))
    run = fused if (mesh.shape["layer"], mesh.shape["feat"]) == (4, 8) else body
    return jax.shard_map(run, mesh=mesh, in_specs=in_specs, out_specs=out_specs, check_vma=False)
```

```python
import functools

import jax
import jax.numpy as jnp
from jax import lax
from jax.experimental import pallas as pl
from jax.experimental.pallas import tpu as pltpu
from jax.sharding import PartitionSpec as P

LEARN_RATE = 4.0
MESH = pl.DeviceIdType.MESH
F32 = jnp.float32
BF16 = jnp.bfloat16

ORDER = (
    ("turn_dec", 0), ("partial", 0), ("pass_tok", 1), ("turn_dec", 1),
    ("pair_sum", 0), ("pass_tok", 2), ("partial", 1), ("pass_tok", 3),
    ("pair_sum", 1), ("activate", 0), ("partial", 2), ("pair_sum", 2),
    ("partial", 3), ("pass_active", 0), ("activate", 1), ("decode", 0),
    ("activate", 2), ("pass_active", 1), ("pair_sum", 3), ("fold", 0),
    ("decode", 1), ("pass_active", 2), ("pass_error", 0), ("decode", 2),
    ("activate", 3), ("fold", 1), ("grad", 0), ("grad_pair", 0),
    ("fold", 2), ("pass_active", 3), ("pass_error", 1), ("decode", 3),
    ("grad", 1), ("pass_error", 2), ("grad_pair", 1), ("fold", 3),
    ("grad", 2), ("pass_error", 3), ("grad_pair", 2), ("grad", 3),
    ("mask", 1), ("grad_pair", 3), ("turn_tok", 0), ("mask", 0),
    ("mask", 2), ("dec_all", 0), ("keep", 0), ("keep", 1),
    ("keep", 2), ("mask", 3), ("keep", 3),
)


def contract_rows(left, right):
    return lax.dot_general(left, right, (((0,), (0,)), ((), ())), preferred_element_type=F32)


def contract_columns(left, right):
    return lax.dot_general(left, right, (((1,), (1,)), ((), ())), preferred_element_type=F32)


def kernel(chunks, rows, quarter, enc_scale, dec_scale, tok_ref, enc_hbm, dec_hbm, bias_ref, dbias_ref,
           tok_t, gp, dec_acc, tok, enc_ref, dec_ref, dec_flat, psend, prec, pown, xsend, xrec, act, rpart, rrec, err,
           gsend, grec, gown, xgsend, xgrec, loads, sends, recvs):
    layer, feat = lax.axis_index("layer"), lax.axis_index("feat")
    xi, core = layer // 2, layer % 2
    pair_dev = (xi * 2 + (1 - core), feat)
    x_dev = ((1 - xi) * 2 + core, feat)
    steps = range(1, 8)
    y_feat = (feat // 2) * 2 + (1 - feat % 2)
    y_dev = (layer, y_feat)

    load_enc = pltpu.make_async_copy(enc_hbm, enc_ref, loads.at[0])
    load_dec = pltpu.make_async_copy(dec_hbm, dec_ref, loads.at[1])
    load_enc.start()
    load_dec.start()

    def feat_at(step):
        return lax.rem(feat + step + 8, 8)

    def feat_dev(step):
        return (layer, feat_at(step))

    barrier = pltpu.get_barrier_semaphore()
    peers = [pair_dev, x_dev] + [feat_dev(step) for step in steps]
    for peer in peers:
        pl.semaphore_signal(barrier, inc=1, device_id=peer, device_id_type=MESH)
    for c in range(chunks):
        tok[c, feat] = tok_ref[c * rows:(c + 1) * rows, :]
    pl.semaphore_wait(barrier, len(peers))

    started = []

    def copy(c, kind, src, dst, dev):
        return pltpu.make_async_remote_copy(
            src_ref=src, dst_ref=dst, send_sem=sends.at[c, kind], recv_sem=recvs.at[c, kind],
            device_id=dev, device_id_type=MESH)

    def send(c, kind, src, dst, dev):
        moving = copy(c, kind, src, dst, dev)
        moving.start()
        started.append(moving)

    def arrive(c, kind, dst, dev):
        copy(c, kind, dst, dst, dev).wait_recv()

    def gather_begin(c, base, buf):
        own = buf.at[c, feat]
        for step in (4, 3, 5, 2, 6, 1, 7):
            send(c, base + step - 1, own, own, feat_dev(step))

    def gather_end(c, base, buf):
        for step in steps:
            arrive(c, base + step - 1, buf.at[c, feat_at(-step)], feat_dev(-step))

    def staged_begin(c, base, buf):
        own = buf.at[c, feat]
        for step in (4, 2, 6):
            send(c, base + step - 1, own, own, feat_dev(step))
        send(c, base, own, own, y_dev)

    def staged_pass(c, base, buf):
        for step in (2, 6, 4):
            slot = buf.at[c, feat_at(-step)]
            arrive(c, base + step - 1, slot, feat_dev(-step))
            send(c, base + step, slot, slot, y_dev)

    def staged_end(c, base, buf):
        arrive(c, base, buf.at[c, y_feat], y_dev)
        for step in (2, 6, 4):
            arrive(c, base + step, buf.at[c, lax.rem(y_feat - step + 8, 8)], y_dev)

    def pass_tok(c):
        staged_pass(c, TOK, tok)

    def pass_error(c):
        staged_pass(c, ERR, err)

    TOK, ERR, RS, PAIR, XP, XA, CA, CB, GP, GX, GM = 0, 7, 14, 21, 23, 24, 25, 26, 27, 29, 31

    def columns(q):
        return pl.ds(pl.multiple_of(q * quarter, quarter), quarter)

    halves = ((0, 1 - xi), (1, xi))

    def partial(c):
        if c == 0:
            gather_end(c, TOK, tok)
        else:
            staged_end(c, TOK, tok)
        if c == 0:
            load_enc.wait()
        x = tok[c].reshape(8 * rows, -1)
        for i, j in halves:
            psend[c, i] = jnp.dot(x, enc_ref[:, columns((1 - core) * 2 + j)], preferred_element_type=F32)
            send(c, PAIR + i, psend.at[c, i], prec.at[c, i], pair_dev)
        for i, j in halves:
            pown[c, i] = jnp.dot(x, enc_ref[:, columns(core * 2 + j)], preferred_element_type=F32)

    def pair_sum(c):
        arrive(c, PAIR, prec.at[c, 0], pair_dev)
        xsend[c] = pown[c, 0] + prec[c, 0]
        send(c, XP, xsend.at[c], xrec.at[c], x_dev)

    def activate(c):
        arrive(c, PAIR + 1, prec.at[c, 1], pair_dev)
        arrive(c, XP, xrec.at[c], x_dev)
        total = pown[c, 1] + prec[c, 1] + xrec[c]
        mine = core * 2 + xi
        preact = enc_scale * total + bias_ref[mine]
        act[c, mine] = jnp.maximum(preact, 0.0).astype(BF16)
        send(c, XA, act.at[c, mine], act.at[c, mine], x_dev)
        send(c, CA, act.at[c, mine], act.at[c, mine], pair_dev)

    def pass_active(c):
        other = act.at[c, core * 2 + (1 - xi)]
        arrive(c, XA, other, x_dev)
        send(c, CB, other, other, pair_dev)

    def decode(c):
        arrive(c, CA, act.at[c, (1 - core) * 2 + xi], pair_dev)
        arrive(c, CB, act.at[c, (1 - core) * 2 + (1 - xi)], pair_dev)
        part = jnp.dot(act[c, 0], dec_flat[0], preferred_element_type=F32)
        for q in range(1, 4):
            part = part + jnp.dot(act[c, q], dec_flat[q], preferred_element_type=F32)
        rpart[c] = (dec_scale * part).astype(BF16).reshape(8, rows, -1)
        for step in (4, 3, 5, 2, 6, 1, 7):
            send(c, RS + step - 1, rpart.at[c, feat_at(step)], rrec.at[c, step - 1], feat_dev(step))

    def fold(c):
        recon = rpart[c, feat].astype(F32)
        for step in steps:
            arrive(c, RS + step - 1, rrec.at[c, step - 1], feat_dev(-step))
            recon = recon + rrec[c, step - 1].astype(F32)
        own = tok_ref[c * rows:(c + 1) * rows, :].astype(F32)
        err[c, feat] = (recon + dbias_ref[...] - own).astype(BF16)
        staged_begin(c, ERR, err)

    def grad(c):
        staged_end(c, ERR, err)
        e = err[c].reshape(8 * rows, -1)
        for j in range(2):
            g = jnp.dot(e, dec_ref[:, columns((1 - core) * 2 + j)], preferred_element_type=F32)
            gsend[c, j] = (dec_scale * g).astype(BF16)
            send(c, GP + j, gsend.at[c, j], grec.at[c, j], pair_dev)
        for j in range(2):
            g = jnp.dot(e, dec_ref[:, columns(core * 2 + j)], preferred_element_type=F32)
            gown[c, j] = dec_scale * g

    def grad_pair(c):
        for j in range(2):
            arrive(c, GP + j, grec.at[c, j], pair_dev)
            both = gown[c, j] + grec[c, j].astype(F32)
            gown[c, j] = both
            xgsend[c, j] = both.astype(BF16)
            send(c, GX + j, xgsend.at[c, j], xgrec.at[c, j], x_dev)

    def mask(c):
        for j in range(2):
            arrive(c, GX + j, xgrec.at[c, j], x_dev)
            whole = gown[c, j] + xgrec[c, j].astype(F32)
            q = core * 2 + j
            lit = act[c, q].astype(F32) > 0.0
            gp[c, q] = jnp.where(lit, whole, 0.0).astype(BF16)
            send(c, GM + j, gp.at[c, q], gp.at[c, q], pair_dev)

    def turn_dec(half):
        if half == 0:
            load_dec.wait()
        for q in (2 * half, 2 * half + 1):
            dec_flat[q] = dec_ref[:, q * quarter:(q + 1) * quarter].T

    def turn_tok(_):
        tok_t[...] = tok[...].reshape(chunks * 8 * rows, -1).T

    def keep(c):
        for j in range(2):
            arrive(c, GM + j, gp.at[c, (1 - core) * 2 + j], pair_dev)

    def dec_all(_):
        left = err[...].reshape(chunks * 8 * rows, -1).T
        for q in range(4):
            right = jnp.concatenate([act[c, q] for c in range(chunks)], axis=0)
            step = jnp.dot(left, right, preferred_element_type=F32)
            dec_acc[:, q * quarter:(q + 1) * quarter] = (-LEARN_RATE * dec_scale * step).astype(BF16)

    gather_begin(0, TOK, tok)
    for c in range(1, chunks):
        staged_begin(c, TOK, tok)
    stages = dict(partial=partial, pair_sum=pair_sum, activate=activate, pass_active=pass_active, decode=decode,
                  fold=fold, grad=grad, grad_pair=grad_pair, mask=mask, dec_all=dec_all, pass_error=pass_error, pass_tok=pass_tok,
                  turn_dec=turn_dec, turn_tok=turn_tok, keep=keep)
    for name, c in ORDER:
        stages[name](c)
    for moving in started:
        moving.wait_send()


def finish(scale, tok_ref, gp_ref, dec_ref, enc_out, dec_out, slabs, sems):
    store_dec = pltpu.make_async_copy(dec_ref, dec_out, sems.at[0])
    store_dec.start()
    quarter = gp_ref.shape[3]
    stores = []
    for q in range(4):
        right = jnp.concatenate([gp_ref[c, q] for c in range(gp_ref.shape[0])], axis=0)
        slabs[q] = (scale * jnp.dot(tok_ref[...], right, preferred_element_type=F32)).astype(BF16)
        store = pltpu.make_async_copy(slabs.at[q], enc_out.at[:, q * quarter:(q + 1) * quarter], sems.at[1 + q])
        store.start()
        stores.append(store)
    for store in [store_dec] + stores:
        store.wait()


def fused(layer_acts, enc_weight, dec_weight, enc_bias, dec_bias):
    tokens, width = layer_acts.shape[1:]
    features = enc_weight.shape[2]
    chunks, quarter = 4, features // 4
    rows = tokens // chunks
    enc_scale = (lax.axis_size("layer") * width) ** (-0.5)
    dec_scale = (features * lax.axis_size("feat")) ** (-0.5)
    whole = 8 * rows
    vmem = pl.BlockSpec(memory_space=pltpu.VMEM)
    anywhere = pl.BlockSpec(memory_space=pl.ANY)
    half32 = pltpu.VMEM((chunks, 2, whole, quarter), F32)
    half16 = pltpu.VMEM((chunks, 2, whole, quarter), BF16)
    quarter32 = pltpu.VMEM((chunks, whole, quarter), F32)
    full16 = pltpu.VMEM((chunks, 4, whole, quarter), BF16)
    blocks = pltpu.VMEM((chunks, 8, rows, width), BF16)
    weights = pltpu.VMEM((width, features), BF16)
    step_shape = jax.ShapeDtypeStruct((width, features), BF16)
    tok_t, gp, dec_step = pl.pallas_call(
        functools.partial(kernel, chunks, rows, quarter, enc_scale, dec_scale),
        out_shape=[
            pltpu.VMEM((width, tokens * 8), BF16),
            full16,
            weights,
        ],
        in_specs=[vmem, anywhere, anywhere, vmem, vmem],
        out_specs=[vmem] * 3,
        scratch_shapes=[
            blocks, weights, weights, pltpu.VMEM((4, quarter, width), BF16), half32, half32, half32, quarter32, quarter32, full16, blocks,
            pltpu.VMEM((chunks, 7, rows, width), BF16),
            blocks, half16, half16, half32, half16, half16,
            pltpu.SemaphoreType.DMA((2,)),
            pltpu.SemaphoreType.DMA((chunks, 33)),
            pltpu.SemaphoreType.DMA((chunks, 33)),
        ],
        compiler_params=pltpu.CompilerParams(
            collective_id=0, has_side_effects=True, vmem_limit_bytes=56 * 2**20),
    )(layer_acts[0], enc_weight[0], jnp.swapaxes(dec_weight[0], 0, 1), enc_bias.reshape(4, 1, quarter), dec_bias)
    enc_step, dec_step = pl.pallas_call(
        functools.partial(finish, -LEARN_RATE * enc_scale),
        out_shape=[step_shape, step_shape],
        in_specs=[vmem] * 3,
        out_specs=[anywhere] * 2,
        scratch_shapes=[pltpu.VMEM((4, width, quarter), BF16), pltpu.SemaphoreType.DMA((5,))],
        compiler_params=pltpu.CompilerParams(vmem_limit_bytes=16 * 2**20),
    )(tok_t, gp, dec_step)
    return enc_step[None], jnp.swapaxes(dec_step, 0, 1)[None]


def body(layer_acts, enc_weight, dec_weight, enc_bias, dec_bias):
    tok_local = layer_acts[0]
    enc_local = enc_weight[0]
    dec_local = dec_weight[0]
    model_width = enc_local.shape[0]
    slab_width = enc_local.shape[1]
    enc_scale = (layer_acts.shape[0] * lax.axis_size("layer") * model_width) ** (-0.5)
    dec_scale = (slab_width * lax.axis_size("feat")) ** (-0.5)
    whole_tokens = lax.all_gather(tok_local, "feat", axis=0, tiled=True)
    partial_value = jnp.dot(whole_tokens, enc_local, preferred_element_type=jnp.float32)
    preact = enc_scale * lax.psum(partial_value, "layer") + enc_bias
    active_b = jnp.maximum(preact, 0.0).astype(jnp.bfloat16)
    recon = lax.psum_scatter(
        dec_scale * jnp.dot(active_b, dec_local, preferred_element_type=jnp.float32),
        "feat",
        scatter_dimension=0,
        tiled=True,
    )
    error_b = (recon + dec_bias[0] - tok_local.astype(jnp.float32)).astype(jnp.bfloat16)
    whole_errors = lax.all_gather(error_b, "feat", axis=0, tiled=True)
    grad_dec = contract_rows(active_b, whole_errors)
    act_terms = dec_scale * contract_columns(whole_errors, dec_local)
    grad_act = lax.psum(act_terms, "layer")
    grad_pre = jnp.where(preact > 0.0, grad_act, 0.0).astype(jnp.bfloat16)
    grad_enc = contract_rows(whole_tokens, grad_pre)
    enc_step = (-LEARN_RATE * enc_scale * grad_enc).astype(jnp.bfloat16)[None]
    dec_step = (-LEARN_RATE * dec_scale * grad_dec).astype(jnp.bfloat16)[None]
    return (enc_step, dec_step)


def solution(mesh):
    in_specs = (
        P("layer", "feat", None),
        P("layer", None, "feat"),
        P("layer", "feat", None),
        P("feat"),
        P("layer", None),
    )
    out_specs = (P("layer", None, "feat"), P("layer", "feat", None))
    run = fused if (mesh.shape["layer"], mesh.shape["feat"]) == (4, 8) else body
    return jax.shard_map(run, mesh=mesh, in_specs=in_specs, out_specs=out_specs, check_vma=False)
```
